32 devices in a mesh: hx: 4 (over y, core), hy: 8 (over z, x).
Axes of the slice: x: 2, y: 2, z: 4, core: 2. Of those that a mesh axis runs over, the one named last changes fastest.
Arguments:
- embeddings: bfloat16 [16384, 768], P(('hx', 'hy')), may hold values from -60 to 60
- bucket: int32 [16384], P(('hx', 'hy')), may hold values from 0 to 63, as said below
Outputs:
- smoothed: bfloat16 [16384, 768], P(('hx', 'hy'))
The draws below stay inside these ranges and needn't reach their ends.
Inputs may be any that keep to these rules, and one draw needn't show every extreme that they name: Every bucket holds at most 512 files and some bucket holds exactly 512; buckets may be empty. The files of each bucket, and of each owner's 2 buckets taken together, lie on the devices as evenly as can be (counts on two devices differ by at most one), so that no device holds more than 32 files of one owner's buckets, and some owner's buckets give exactly 32 to every device.
All inputs are finite; a program needn't handle non-finite values.
Results may differ from the reference program's by a relative error of at most 0.0042.
Values may be sent and summed in bfloat16 or wider, within the bound.
No kernel may reach another device: no remote copies, remote signals or barrier semaphores. Data moves between devices by JAX's collectives and lax.ppermute only.
A program may use at most 64 MiB of HBM per device.

```python
import math
import jax
import jax.numpy as jnp
from jax import lax

D = 768
BPD = 2
F_DEV = 512
CAP = 512
FILES = 16384
N_HX = 4
N_HY = 8


def draw_bucket(key, part):
    devices_all = N_HX * N_HY
    bucket_total = BPD * devices_all
    half_cap = CAP // 2
    key_owner = jax.random.fold_in(key, 11)
    key_split = jax.random.fold_in(key, 12)
    key_place = jax.random.fold_in(key, 13)
    owner_perm = jax.random.permutation(key_owner, devices_all)
    shifts = jax.random.randint(key_split, (devices_all // 2, BPD), -half_cap, half_cap + 1)
    shifts = shifts.at[0].set(half_cap)
    counts = jnp.zeros((devices_all, BPD), jnp.int32)
    counts = counts.at[owner_perm[0::2]].set(half_cap + shifts)
    counts = counts.at[owner_perm[1::2]].set(half_cap - shifts)
    counts = counts.reshape(bucket_total)
    listing = jnp.repeat(jnp.arange(bucket_total, dtype=jnp.int32), counts, total_repeat_length=FILES)
    per_device = listing.reshape(F_DEV, devices_all).T
    row_keys = jax.random.split(key_place, devices_all)
    orders = jax.vmap(lambda single: jax.random.permutation(single, F_DEV))(row_keys)
    per_device = jnp.take_along_axis(per_device, orders, axis=1)
    return per_device.reshape(FILES).astype(jnp.int32)


def draw_embeddings(key, part):
    key_base = jax.random.fold_in(key, 21)
    key_rows = jax.random.fold_in(key, 22)
    key_cols = jax.random.fold_in(key, 23)
    row_scale = jnp.exp(jax.random.uniform(key_rows, (FILES, 1), jnp.float32) * math.log(10.0))
    col_scale = jnp.exp(jax.random.uniform(key_cols, (1, D), jnp.float32) * math.log(10.0))
    base = jnp.clip(jax.random.normal(key_base, (FILES, D), jnp.float32), -6.0, 6.0)
    return (base * row_scale * col_scale / 10.0).astype(jnp.bfloat16)


def setup_inputs(seed: int = 0) -> dict:
    streams_of = jax.random.split(jax.random.key(seed), 3)
    return {
        "embeddings": draw_embeddings(jax.random.fold_in(streams_of[2], 71), 0),
        "bucket": draw_bucket(jax.random.fold_in(streams_of[2], 71), 0),
    }


sharpness = 32.0
epsilon = 1e-06

def inverse_norm(rows):
    return 1.0 / jnp.sqrt(lax.optimization_barrier(jnp.mean(jnp.square(rows.astype(jnp.float32)), axis=-1)) + epsilon)

def reference(embeddings, bucket):
    total_files = embeddings.shape[0]
    bucket_count = BPD * N_HX * N_HY
    file_index = jnp.arange(total_files, dtype=jnp.int32)
    file_order = jnp.argsort(bucket * total_files + file_index).astype(jnp.int32)
    sorted_bucket = bucket[file_order].astype(jnp.int32)
    per_bucket = jnp.zeros((bucket_count,), jnp.int32).at[bucket].add(1)
    starts = (jnp.cumsum(per_bucket) - per_bucket).astype(jnp.int32)
    rank_sorted = (file_index - starts[sorted_bucket]).astype(jnp.int32)
    block_rows = jnp.zeros((bucket_count, CAP, D), embeddings.dtype).at[sorted_bucket, rank_sorted].set(embeddings[file_order])
    block_file = jnp.full((bucket_count, CAP), -1, jnp.int32).at[sorted_bucket, rank_sorted].set(file_order)
    block_inv = jnp.zeros((bucket_count, CAP), jnp.float32).at[sorted_bucket, rank_sorted].set(inverse_norm(embeddings)[file_order])
    high_x = N_HX // 2 * N_HY * BPD
    high_y = N_HY // 2 * BPD

    def one_bucket(which):
        probes = jnp.stack([which, which ^ 1, which ^ high_x, which ^ high_y]).astype(jnp.int32)
        key_rows = block_rows[probes].reshape(4 * CAP, D)
        key_inv = block_inv[probes].reshape(4 * CAP)
        key_file = block_file[probes].reshape(4 * CAP)
        query_rows = block_rows[which]
        query_inv = block_inv[which]
        query_file = block_file[which]
        products = jnp.dot(query_rows, key_rows.T, preferred_element_type=jnp.float32)
        score = products * query_inv[:, None] * key_inv[None, :] * (sharpness / D)
        live = (key_file[None, :] >= 0) & (key_file[None, :] != query_file[:, None])
        kernel = jnp.where(live, jnp.exp(score), jnp.float32(0.0))
        kernel_low = kernel.astype(jnp.bfloat16)
        numerator = jnp.dot(kernel_low, key_rows, preferred_element_type=jnp.float32)
        denominator = 1.0 + lax.optimization_barrier(jnp.sum(kernel, axis=1))
        return (numerator / denominator[:, None]).astype(jnp.bfloat16)
    out_blocks = lax.map(one_bucket, jnp.arange(bucket_count, dtype=jnp.int32))
    rank_file = jnp.zeros((total_files,), jnp.int32).at[file_order].set(rank_sorted)
    return out_blocks[bucket, rank_file]
```

```python
import jax
import jax.numpy as jnp
from jax import lax
from jax.sharding import PartitionSpec as P

BPD = 2
CAP = 512
META = 16

sharpness = 32.0
epsilon = 1e-06

AXES = ("hx", "hy")


def swapped(value, bit, total):
    return lax.ppermute(value, AXES, [(i, i ^ bit) for i in range(total)])


def exchange(value, groups):
    return lax.all_to_all(
        value, AXES, split_axis=0, concat_axis=0, tiled=True, axis_index_groups=groups
    )


def match_of(target, total):
    return jnp.arange(total, dtype=jnp.int32)[:, None] == target[None, :]


def pick(match, rows):
    return jnp.dot(match, rows, preferred_element_type=jnp.float32).astype(jnp.bfloat16)


def attend(queries, query_inv, query_bits, keys, key_inv, key_bit, factor, exclude_self):
    products = lax.dot_general(
        queries, keys, (((1,), (1,)), ((), ())), preferred_element_type=jnp.float32
    )
    score = products * query_inv[:, None] * key_inv[None, :] * factor
    live = (query_bits[:, None] & key_bit[None, :]) != 0
    if exclude_self:
        row = jnp.arange(queries.shape[0], dtype=jnp.int32)
        live = live & (row[:, None] != row[None, :])
    kernel = jnp.where(live, jnp.exp(score), jnp.float32(0.0))
    numerator = jnp.dot(kernel.astype(jnp.bfloat16), keys, preferred_element_type=jnp.float32)
    return numerator, jnp.sum(kernel, axis=1)


def key_facts(meta):
    wide = meta.astype(jnp.float32)
    tag = wide[:, 0].astype(jnp.int32)
    inv = wide[:, 1] + wide[:, 2] + wide[:, 3]
    bit = jnp.where(tag > 0, jnp.left_shift(1, jnp.maximum(tag - 1, 0)), 0)
    return tag, inv, bit


def body(embeddings, bucket):
    nx, ny = lax.axis_size("hx"), lax.axis_size("hy")
    devices = nx * ny
    cells = devices // 4
    files, width = embeddings.shape
    slots = 4 * BPD * CAP // devices
    slots_a = max(16, slots * 3 // 4 // 16 * 16)
    slots_b = slots - slots_a
    stride = slots // slots_b
    files_a = files - files // stride
    core_bit, half_bit = ny, ny // 2
    groups = [
        [(2 * u + core) * ny + half * (ny // 2) + v for u in range(nx // 2) for v in range(ny // 2)]
        for core in range(2)
        for half in range(2)
    ]

    a, b, c = bucket // (BPD * ny), bucket // BPD % ny, bucket % BPD
    cell = a % (nx // 2) * (ny // 2) + b % (ny // 2)
    tag = a // (nx // 2) * 4 + b // (ny // 2) * 2 + c
    order = cell * files + jnp.arange(files, dtype=jnp.int32)
    rank = jnp.sum((order[:, None] < order[None, :]).astype(jnp.int32), axis=0)
    start = jnp.sum((cell[:, None] < cell[None, :]).astype(jnp.int32), axis=0)
    late = rank % stride == stride - 1
    late_rank, late_start = rank // stride, start // stride
    early_index = (rank - late_rank) - (start - late_start)
    slot = cell * slots + jnp.where(late, slots_a + late_rank - late_start, early_index)

    early_match = match_of(jnp.where(late, files, rank - late_rank), files_a)
    early_rows = pick(early_match.astype(jnp.bfloat16), embeddings)
    early_slot = jnp.sum(
        jnp.where(early_match, (cell * slots_a + early_index)[None, :], 0), axis=1
    )
    other_early = swapped(early_rows, half_bit, devices)
    other_slot = swapped(early_slot, half_bit, devices)

    squares = jnp.square(embeddings.astype(jnp.float32))
    inv = 1.0 / jnp.sqrt(jnp.mean(squares, axis=-1) + epsilon)
    high = lax.reduce_precision(inv, 8, 7)
    middle = lax.reduce_precision(inv - high, 8, 7)
    low = inv - high - middle
    facts = jnp.stack([(tag + 1).astype(jnp.float32), high, middle, low]).astype(jnp.bfloat16)
    facts = jnp.pad(facts, ((0, META - 4), (0, 0)))
    send_match = match_of(slot, cells * slots).astype(jnp.bfloat16)
    send_rows = pick(send_match, embeddings).reshape(cells, slots, width)
    send_meta = lax.dot_general(
        facts, send_match, (((1,), (1,)), ((), ())), preferred_element_type=jnp.float32
    ).astype(jnp.bfloat16)
    send_meta = send_meta.reshape(META, cells, slots).transpose(1, 0, 2)
    send_meta = jnp.pad(send_meta, ((0, 0), (0, 0), (0, width - slots)))
    got = exchange(jnp.concatenate([send_rows, send_meta], axis=1), groups)
    own_rows = got[:, :slots].reshape(cells * slots, width)
    own_meta = got[:, slots:, :slots]

    half_late = swapped(got[:, slots_a:slots], half_bit, devices).reshape(cells * slots_b, width)
    half_meta = swapped(own_meta, half_bit, devices)

    other_match = match_of(other_slot, cells * slots_a).astype(jnp.bfloat16)
    half_early = exchange(
        pick(other_match, other_early).reshape(cells, slots_a, width), groups
    ).reshape(cells * slots_a, width)

    mate_rows = swapped(own_rows, core_bit, devices)
    mate_meta, mate_half_meta = (
        swapped(own_meta, core_bit, devices),
        swapped(half_meta, core_bit, devices),
    )
    mate_late = swapped(half_late, core_bit, devices)
    mate_early = swapped(half_early, core_bit, devices)

    own_tag, own_inv, own_bit = key_facts(own_meta)
    query_tag = jnp.maximum(own_tag - 1, 0)
    query_bits = (
        jnp.left_shift(1, query_tag)
        | jnp.left_shift(1, query_tag ^ 1)
        | jnp.left_shift(1, query_tag ^ 2)
        | jnp.left_shift(1, query_tag ^ 4)
    )
    query_inv, query_bits = own_inv.reshape(-1), query_bits.reshape(-1)
    key_sets = [(own_rows, own_inv, own_bit, True)]
    _, mate_inv, mate_bit = key_facts(mate_meta)
    key_sets.append((mate_rows, mate_inv, mate_bit, False))
    for meta, early, late_rows in (
        (half_meta, half_early, half_late),
        (mate_half_meta, mate_early, mate_late),
    ):
        _, one_inv, one_bit = key_facts(meta)
        key_sets.append((late_rows, one_inv[:, slots_a:], one_bit[:, slots_a:], False))
        key_sets.append((early, one_inv[:, :slots_a], one_bit[:, :slots_a], False))
    factor = sharpness / width
    numerator = jnp.zeros((cells * slots, width), jnp.float32)
    denominator = jnp.ones((cells * slots,), jnp.float32)
    for keys, key_inv, key_bit, is_own in key_sets:
        one_numerator, one_denominator = attend(
            own_rows, query_inv, query_bits, keys, key_inv.reshape(-1), key_bit.reshape(-1), factor, is_own
        )
        numerator, denominator = numerator + one_numerator, denominator + one_denominator
    smoothed = (numerator / denominator[:, None]).astype(jnp.bfloat16)
    home = exchange(smoothed.reshape(cells, slots, width), groups).reshape(cells * slots, width)
    return lax.dot_general(
        send_match, home, (((0,), (0,)), ((), ())), preferred_element_type=jnp.float32
    ).astype(jnp.bfloat16)


def solution(mesh):
    return jax.shard_map(
        body,
        mesh=mesh,
        in_specs=(P(("hx", "hy"), None), P(("hx", "hy"))),
        out_specs=P(("hx", "hy"), None),
        check_vma=False,
    )
```

```python
import functools

import jax
import jax.numpy as jnp
from jax import lax
from jax.experimental import pallas as pl
from jax.experimental.pallas import tpu as pltpu
from jax.sharding import PartitionSpec as P

BPD = 2
CAP = 512
META = 16
FACTS = 4
LANES = 128

sharpness = 32.0
epsilon = 1e-06

AXES = ("hx", "hy")
VMEM = pl.BlockSpec(memory_space=pltpu.VMEM)
ANY = pl.BlockSpec(memory_space=pl.ANY)
F32, BF16, I32 = jnp.float32, jnp.bfloat16, jnp.int32


class Plan:
    def __init__(self, nx, ny, files, width):
        self.nx, self.ny, self.files, self.width = nx, ny, files, width
        self.devices = nx * ny
        self.cells = self.devices // 4
        self.slots = 4 * BPD * CAP // self.devices
        self.slots_a = max(16, self.slots * 3 // 4 // 16 * 16)
        self.slots_b = self.slots - self.slots_a
        self.stride = self.slots // self.slots_b
        self.files_a = files - files // self.stride
        self.total = self.cells * self.slots
        self.segments = width // LANES
        self.block = max(META, -(-(-(-FACTS * self.cells // self.segments)) // META) * META)
        self.core_bit, self.half_bit = ny, ny // 2
        self.groups = [
            [(2 * u + core) * ny + half * (ny // 2) + v for u in range(nx // 2) for v in range(ny // 2)]
            for core in range(2)
            for half in range(2)
        ]


def swapped(value, bit, plan):
    return lax.ppermute(value, AXES, [(i, i ^ bit) for i in range(plan.devices)])


def exchange(value, plan):
    return lax.all_to_all(
        value, AXES, split_axis=0, concat_axis=0, tiled=True, axis_index_groups=plan.groups
    )


def call(kernel, out_shape, in_specs, flops, moved, exps=0):
    return pl.pallas_call(
        kernel,
        out_shape=out_shape,
        in_specs=in_specs,
        out_specs=jax.tree.map(lambda _: VMEM, out_shape),
        compiler_params=pltpu.CompilerParams(vmem_limit_bytes=56 * 1024 * 1024),
        cost_estimate=pl.CostEstimate(flops=flops, bytes_accessed=moved, transcendentals=exps),
    )


def iota(shape, dim):
    return lax.broadcasted_iota(I32, shape, dim)


def column(row):
    return jnp.broadcast_to(row, (LANES, row.shape[1])).T


def rows_dot(left, right):
    return lax.dot_general(left, right, (((1,), (1,)), ((), ())), preferred_element_type=F32)


def sort_kernel(plan, bucket_ref, rows_ref, early_ref, place_ref):
    nx, ny, files = plan.nx, plan.ny, plan.files
    bucket = bucket_ref[...]
    low_b = ny.bit_length() - 1
    a = bucket >> (low_b + 1)
    b = (bucket >> 1) & (ny - 1)
    c = bucket & 1
    cell = (a & (nx // 2 - 1)) * (ny // 2) + (b & (ny // 2 - 1))
    tag = (a >> (nx.bit_length() - 2)) * 4 + (b >> (low_b - 1)) * 2 + c + 1
    order = cell * files + iota((1, files), 1)
    rank = jnp.sum((column(order)[:, :1] < order).astype(I32), axis=0, keepdims=True)
    start = jnp.sum((column(cell)[:, :1] < cell).astype(I32), axis=0, keepdims=True)
    shift = plan.stride.bit_length() - 1
    late = (rank & (plan.stride - 1)) == plan.stride - 1
    late_rank, late_start = rank >> shift, start >> shift
    early_index = (rank - late_rank) - (start - late_start)
    slot = cell * plan.slots + jnp.where(late, plan.slots_a + late_rank - late_start, early_index)
    place_ref[...] = jnp.zeros(place_ref.shape, I32)
    place_ref[0:1, :] = slot
    place_ref[1:2, :] = tag
    target = jnp.where(late, files, rank - late_rank)
    match = (iota((plan.files_a, files), 0) == target).astype(F32).astype(BF16)
    early_ref[0 : plan.files_a, :] = jnp.dot(
        match, rows_ref[...], preferred_element_type=F32
    ).astype(BF16)
    which = iota((META, files), 0)
    info = jnp.where(which == 0, cell, jnp.where(which == 1, early_index, 0))
    info = rows_dot(info.astype(F32).astype(BF16), match).astype(BF16)
    early_ref[plan.files_a :, :] = jnp.zeros((META, plan.width), BF16)
    early_ref[plan.files_a :, 0 : plan.files_a] = info


def send_kernel(plan, place_ref, rows_ref, after_ref, out_ref):
    del after_ref
    files, slots = plan.files, plan.slots
    slot, tag = place_ref[0:1, :], place_ref[1:2, :]
    rows = rows_ref[...]
    wide = rows.astype(F32)
    square = jnp.sum(wide * wide, axis=1, keepdims=True)
    square = jnp.broadcast_to(square, (files, LANES)).T[0:1, :]
    inv = 1.0 / jnp.sqrt(square * (1.0 / plan.width) + epsilon)
    high = inv.astype(BF16).astype(F32)
    middle = (inv - high).astype(BF16).astype(F32)
    low = inv - high - middle
    which = iota((META, files), 0)
    facts = jnp.where(
        which == 0,
        tag.astype(F32),
        jnp.where(which == 1, high, jnp.where(which == 2, middle, jnp.where(which == 3, low, 0.0))),
    ).astype(BF16)
    for cell in range(plan.cells):
        match = (iota((slots, files), 0) + cell * slots == slot).astype(F32).astype(BF16)
        out_ref[cell, 0:slots, :] = jnp.dot(match, rows, preferred_element_type=F32).astype(BF16)
        out_ref[cell, slots:, :] = jnp.zeros((META, plan.width), BF16)
        out_ref[cell, slots:, 0:slots] = rows_dot(facts, match).astype(BF16)


def split_kernel(plan, got_ref, rows_ref, late_ref):
    slots, slots_a, slots_b, cells = plan.slots, plan.slots_a, plan.slots_b, plan.cells
    for source in range(cells):
        rows_ref[source * slots : (source + 1) * slots, :] = got_ref[source, 0:slots, :]
        late_ref[source * slots_b : (source + 1) * slots_b, :] = got_ref[source, slots_a:slots, :]
    metas = [got_ref[source, slots:, 0:LANES].astype(F32) for source in range(cells)]
    for segment in range(plan.segments):
        lines = []
        for line in range(plan.block):
            fact, source = divmod(line * plan.segments + segment, cells)
            lines.append(
                metas[source][fact : fact + 1, :] if fact < FACTS else jnp.zeros((1, LANES), F32)
            )
        block = jnp.concatenate(lines, axis=0).astype(BF16)
        lanes = slice(segment * LANES, (segment + 1) * LANES)
        rows_ref[cells * slots :, lanes] = block
        late_ref[cells * slots_b :, lanes] = block


def relay_kernel(plan, early_ref, after_ref, out_ref):
    del after_ref
    files_a = plan.files_a
    info = early_ref[files_a:, 0:files_a].astype(F32)
    target = (info[0:1, :] * plan.slots_a + info[1:2, :]).astype(I32)
    rows = early_ref[0:files_a, :]
    for cell in range(plan.cells):
        match = iota((plan.slots_a, files_a), 0) + cell * plan.slots_a == target
        out_ref[cell] = jnp.dot(
            match.astype(F32).astype(BF16), rows, preferred_element_type=F32
        ).astype(BF16)


def attend_kernel(plan, sets, first, last, *refs):
    refs = list(refs)
    query_ref, fact_ref = refs.pop(0), refs.pop(0)
    keys = [(refs.pop(0), refs.pop(0), count, own) for count, own in sets]
    if not first:
        old_ref, old_sum_ref = refs.pop(0), refs.pop(0)
    if last:
        out_ref, column_ref = refs
    else:
        out_ref, sum_ref, column_ref = refs
    tag = fact_ref[0:1, :].astype(I32)
    place = jnp.maximum(tag - 1, 0)
    bits = (2 << place) | (2 << (place ^ 1)) | (2 << (place ^ 2)) | (2 << (place ^ 4))
    column_ref[0] = column(fact_ref[1:2, :] * (sharpness / plan.width))
    column_ref[1] = column(bits.astype(F32))
    chunk = 256

    @pl.loop(0, plan.total // chunk)
    def _(step):
        here = pl.ds(pl.multiple_of(step * chunk, chunk), chunk)
        query = query_ref[here, :]
        query_inv = column_ref[0, here, :][:, 0:1]
        query_bits = column_ref[1, here, :][:, 0:1].astype(I32)
        if first:
            numerator = jnp.zeros((chunk, plan.width), F32)
            denominator = jnp.ones((chunk, LANES), F32)
        else:
            numerator, denominator = old_ref[here, :], old_sum_ref[here, :]
        for key_ref, key_fact_ref, count, own in keys:
            for begin in range(0, count, 512):
                size = min(512, count - begin)
                lanes = slice(begin, begin + size)
                key = key_ref[lanes, :]
                key_bit = 1 << key_fact_ref[0:1, lanes].astype(I32)
                score = rows_dot(query, key) * query_inv * key_fact_ref[1:2, lanes]
                live = (query_bits & key_bit) != 0
                if own:
                    live = live & (
                        iota((chunk, size), 0) + (step * chunk - begin) != iota((chunk, size), 1)
                    )
                kernel = jnp.where(live, jnp.exp(score), 0.0)
                denominator = denominator + jnp.sum(kernel, axis=1, keepdims=True)
                numerator = numerator + jnp.dot(
                    kernel.astype(BF16), key, preferred_element_type=F32
                )
        if last:
            out_ref[here, :] = (numerator / denominator[:, 0:1]).astype(BF16)
        else:
            out_ref[here, :] = numerator
            sum_ref[here, :] = denominator


def attend(plan, query, facts, key_sets, old=None, last=False):
    sets = [(fact.shape[1], own) for _, fact, own in key_sets]
    total, width = plan.total, plan.width
    keys = sum(count for count, _ in sets)
    if last:
        out_shape = jax.ShapeDtypeStruct((total, width), BF16)
    else:
        out_shape = (
            jax.ShapeDtypeStruct((total, width), F32),
            jax.ShapeDtypeStruct((total, LANES), F32),
        )
    args = [query, facts]
    for rows, fact, _ in key_sets:
        args += [rows, fact]
    if old is not None:
        args += list(old)
    return pl.pallas_call(
        functools.partial(attend_kernel, plan, sets, old is None, last),
        out_shape=out_shape,
        in_specs=[VMEM] * len(args),
        out_specs=jax.tree.map(lambda _: VMEM, out_shape),
        scratch_shapes=[pltpu.VMEM((2, total, LANES), F32)],
        compiler_params=pltpu.CompilerParams(vmem_limit_bytes=56 * 1024 * 1024),
        cost_estimate=pl.CostEstimate(
            flops=4 * total * keys * width, bytes_accessed=12 * total * width, transcendentals=total * keys
        ),
    )(*args)


def unpack_kernel(plan, place_ref, home_ref, out_ref):
    slot = column(place_ref[0:1, :])[:, 0:1]
    match = (iota((plan.files, plan.total), 1) == slot).astype(F32).astype(BF16)
    out_ref[...] = jnp.dot(match, home_ref[...], preferred_element_type=F32).astype(BF16)


def key_facts(plan, block):
    wide = block.reshape(plan.block * plan.segments, LANES)[: FACTS * plan.cells]
    wide = wide.reshape(FACTS, plan.cells, LANES)[:, :, : plan.slots].astype(F32)
    return jnp.stack([wide[0], wide[1] + wide[2] + wide[3]])


def flat(facts):
    return facts.reshape(2, -1)


def body(embeddings, bucket):
    files, width = embeddings.shape
    plan = Plan(lax.axis_size("hx"), lax.axis_size("hy"), files, width)
    cells, slots, slots_a, total = plan.cells, plan.slots, plan.slots_a, plan.total
    row_bytes = width * 2

    early, place = call(
        functools.partial(sort_kernel, plan),
        (
            jax.ShapeDtypeStruct((plan.files_a + META, width), BF16),
            jax.ShapeDtypeStruct((8, files), I32),
        ),
        [VMEM, VMEM],
        2 * plan.files_a * files * width,
        2 * files * row_bytes,
    )(bucket.reshape(1, files), embeddings)
    other_early = swapped(early, plan.half_bit, plan)
    payload = call(
        functools.partial(send_kernel, plan),
        jax.ShapeDtypeStruct((cells, slots + META, width), BF16),
        [VMEM, VMEM, ANY],
        2 * total * files * width,
        3 * files * row_bytes,
    )(place, embeddings, early)
    got = exchange(payload, plan)
    own, late = call(
        functools.partial(split_kernel, plan),
        (
            jax.ShapeDtypeStruct((total + plan.block, width), BF16),
            jax.ShapeDtypeStruct((cells * plan.slots_b + plan.block, width), BF16),
        ),
        [VMEM],
        0,
        4 * total * row_bytes,
    )(got)
    half_late = swapped(late, plan.half_bit, plan)
    mate = swapped(own, plan.core_bit, plan)
    mate_late = swapped(half_late, plan.core_bit, plan)

    own_facts = flat(key_facts(plan, own[total:]))
    sums = attend(plan, own, own_facts, [(own, own_facts, True)])
    relayed = call(
        functools.partial(relay_kernel, plan),
        jax.ShapeDtypeStruct((cells, slots_a, width), BF16),
        [VMEM, ANY],
        2 * cells * slots_a * plan.files_a * width,
        2 * cells * slots_a * row_bytes,
    )(other_early, sums[1])
    half_early = exchange(relayed, plan).reshape(cells * slots_a, width)
    sums = attend(plan, own, own_facts, [(mate, flat(key_facts(plan, mate[total:])), False)], sums)
    mate_early = swapped(half_early, plan.core_bit, plan)

    late_rows = cells * plan.slots_b
    half_facts = key_facts(plan, half_late[late_rows:])
    mate_facts = key_facts(plan, mate_late[late_rows:])
    sums = attend(
        plan,
        own,
        own_facts,
        [
            (half_late, flat(half_facts[:, :, slots_a:]), False),
            (mate_late, flat(mate_facts[:, :, slots_a:]), False),
            (half_early, flat(half_facts[:, :, :slots_a]), False),
        ],
        sums,
    )
    smoothed = attend(
        plan, own, own_facts, [(mate_early, flat(mate_facts[:, :, :slots_a]), False)], sums, last=True
    )
    home = exchange(smoothed.reshape(cells, slots, width), plan).reshape(total, width)
    return call(
        functools.partial(unpack_kernel, plan),
        jax.ShapeDtypeStruct((files, width), BF16),
        [VMEM, VMEM],
        2 * total * files * width,
        3 * files * row_bytes,
    )(place, home)


def solution(mesh):
    return jax.shard_map(
        body,
        mesh=mesh,
        in_specs=(P(("hx", "hy"), None), P(("hx", "hy"))),
        out_specs=P(("hx", "hy"), None),
        check_vma=False,
    )
```

```python
import functools
import math

import jax
import jax.numpy as jnp
from jax import lax
from jax.experimental import pallas as pl
from jax.experimental.pallas import tpu as pltpu
from jax.sharding import PartitionSpec as P

BPD = 2
CAP = 512
TILE = 16
FACTS = 4
LANES = 128

sharpness = 32.0
epsilon = 1e-06

AXES = ("hx", "hy")
VMEM = pl.BlockSpec(memory_space=pltpu.VMEM)
ANY = pl.BlockSpec(memory_space=pl.ANY)
F32, BF16, I32 = jnp.float32, jnp.bfloat16, jnp.int32


class Plan:
    def __init__(self, nx, ny, files, width, slots):
        self.nx, self.ny, self.files, self.width, self.slots = nx, ny, files, width, slots
        self.devices = nx * ny
        self.cells = self.devices // 4
        self.total = self.cells * slots
        self.known = min(slots, LANES)
        self.core_bit, self.half_bit = ny, ny // 2
        self.groups = [
            [(2 * u + core) * ny + half * (ny // 2) + v for u in range(nx // 2) for v in range(ny // 2)]
            for core in range(2)
            for half in range(2)
        ]


def swapped(value, bit, plan):
    return lax.ppermute(value, AXES, [(i, i ^ bit) for i in range(plan.devices)])


def exchange(value, plan):
    shape = (plan.cells, plan.slots, plan.width)
    return lax.all_to_all(
        value.reshape(shape), AXES, split_axis=0, concat_axis=0, tiled=True, axis_index_groups=plan.groups
    ).reshape(plan.total, plan.width)


def call(kernel, out_shape, args, flops, moved, exps=0, after=(), scratch=()):
    return pl.pallas_call(
        kernel,
        out_shape=out_shape,
        in_specs=[VMEM] * len(args) + [ANY] * len(after),
        out_specs=jax.tree.map(lambda _: VMEM, out_shape),
        scratch_shapes=list(scratch),
        compiler_params=pltpu.CompilerParams(vmem_limit_bytes=56 * 1024 * 1024),
        cost_estimate=pl.CostEstimate(flops=flops, bytes_accessed=moved, transcendentals=exps),
    )(*args, *after)


def iota(shape, dim):
    return lax.broadcasted_iota(I32, shape, dim)


def column(row):
    return jnp.broadcast_to(row, (LANES, row.shape[1])).T


def rows_dot(left, right):
    return lax.dot_general(left, right, (((1,), (1,)), ((), ())), preferred_element_type=F32)


def as_bf16(mask):
    return mask.astype(F32).astype(BF16)


def pack_kernel(plan, bucket_ref, rows_ref, *refs):
    out_ref, place_ref = refs[-2:]
    nx, ny, files, slots, known = plan.nx, plan.ny, plan.files, plan.slots, plan.known
    bucket = bucket_ref[...]
    low_b = ny.bit_length() - 1
    a = bucket >> (low_b + 1)
    b = (bucket >> 1) & (ny - 1)
    c = bucket & 1
    cell = (a & (nx // 2 - 1)) * (ny // 2) + (b & (ny // 2 - 1))
    tag = (a >> (nx.bit_length() - 2)) * 4 + (b >> (low_b - 1)) * 2 + c + 1
    order = cell * files + iota((1, files), 1)
    before = column(order)[:, :1] < order
    same = column(cell)[:, :1] == cell
    index = jnp.sum((before & same).astype(I32), axis=0, keepdims=True)
    over = jnp.max(index, axis=1, keepdims=True) >= slots - 1
    slot = jnp.where(index < slots - 1, cell * slots + index, plan.total)
    place_ref[...] = jnp.broadcast_to(slot, place_ref.shape)

    rows = rows_ref[...]
    wide = rows.astype(F32)
    square = jnp.sum(wide * wide, axis=1, keepdims=True)
    square = jnp.broadcast_to(square, (files, LANES)).T[0:1, :]
    inv = 1.0 / jnp.sqrt(square * (1.0 / plan.width) + epsilon)
    high = inv.astype(BF16).astype(F32)
    middle = (inv - high).astype(BF16).astype(F32)
    low = inv - high - middle
    which = iota((TILE, files), 0)
    facts = jnp.where(
        which == 0,
        tag.astype(F32),
        jnp.where(which == 1, high, jnp.where(which == 2, middle, jnp.where(which == 3, low, 0.0))),
    ).astype(BF16)
    last = iota((TILE, known), 0) == TILE - 1
    flag = jnp.broadcast_to(over.astype(F32), (TILE, LANES))
    for block in range(plan.cells):
        match = as_bf16(iota((slots, files), 0) + block * slots == slot)
        packed = jnp.dot(match, rows, preferred_element_type=F32)
        here = block * slots
        out_ref[here : here + slots, :] = packed.astype(BF16)
        line = rows_dot(facts, match)
        tail = slice(here + slots - TILE, here + slots)
        for fact in range(FACTS):
            lanes = slice(fact * LANES, fact * LANES + known)
            out_ref[tail, lanes] = jnp.where(
                last, line[fact : fact + 1, :known], packed[slots - TILE :, lanes]
            ).astype(BF16)
        lanes = slice(FACTS * LANES, (FACTS + 1) * LANES)
        out_ref[tail, lanes] = jnp.where(
            iota((TILE, LANES), 0) == TILE - 1, flag, packed[slots - TILE :, lanes]
        ).astype(BF16)


def facts_of(plan, ref):
    slots, known = plan.slots, plan.known
    tags, invs = [], []
    for source in range(plan.cells):
        end = (source + 1) * slots
        lines = ref[end - TILE : end, 0 : FACTS * LANES].astype(F32)[TILE - 1 : TILE, :]
        tag, high, middle, low = (
            lines[:, fact * LANES : fact * LANES + known] for fact in range(FACTS)
        )
        tags.append(tag)
        invs.append(high + middle + low)
        if known < slots:
            empty = jnp.zeros((1, slots - known), F32)
            tags.append(empty)
            invs.append(empty)
    return jnp.concatenate(tags, axis=1), jnp.concatenate(invs, axis=1)


def attend_kernel(plan, sets, first, last, *refs):
    refs = list(refs)
    query_ref = refs.pop(0)
    keys = [(refs.pop(0), own) for own in sets]
    if not first:
        old_ref, old_sum_ref = refs.pop(0), refs.pop(0)
    if last:
        out_ref, column_ref = refs
    else:
        out_ref, sum_ref, column_ref = refs
    total, width = plan.total, plan.width
    tag, inv = facts_of(plan, query_ref)
    place = jnp.maximum(tag.astype(I32) - 1, 0)
    bits = (2 << place) | (2 << (place ^ 1)) | (2 << (place ^ 2)) | (2 << (place ^ 4))
    column_ref[0] = column(inv * (sharpness / width * math.log2(math.e)))
    column_ref[1] = column(bits.astype(F32))
    key_facts = []
    for key_ref, own in keys:
        key_tag, key_inv = facts_of(plan, key_ref)
        key_facts.append((1 << key_tag.astype(I32), key_inv))
    chunk = total // 2
    for step in range(2):
        here = slice(step * chunk, (step + 1) * chunk)
        query = query_ref[here, :]
        query_inv = column_ref[0, here, :][:, 0:1]
        query_bits = column_ref[1, here, :][:, 0:1].astype(I32)
        if first:
            numerator = jnp.zeros((chunk, width), F32)
            denominator = jnp.ones((chunk, LANES), F32)
        else:
            numerator, denominator = old_ref[here, :], old_sum_ref[here, :]
        for (key_ref, own), (key_bit, key_inv) in zip(keys, key_facts):
            score = rows_dot(query, key_ref[...]) * query_inv * key_inv
            live = (query_bits & key_bit) != 0
            if own:
                live = live & (iota((chunk, total), 0) + step * chunk != iota((chunk, total), 1))
            kernel = jnp.where(live, jnp.exp2(score), 0.0)
            denominator = denominator + jnp.sum(kernel, axis=1, keepdims=True)
            numerator = numerator + jnp.dot(
                kernel.astype(BF16), key_ref[...], preferred_element_type=F32
            )
        if last:
            out_ref[here, :] = (numerator / denominator[:, 0:1]).astype(BF16)
        else:
            out_ref[here, :] = numerator
            sum_ref[here, :] = denominator


def attend(plan, query, key_sets, old=(), last=False):
    total, width = plan.total, plan.width
    count = len(key_sets) * total
    if last:
        out_shape = jax.ShapeDtypeStruct((total, width), BF16)
    else:
        out_shape = (
            jax.ShapeDtypeStruct((total, width), F32),
            jax.ShapeDtypeStruct((total, LANES), F32),
        )
    return call(
        functools.partial(attend_kernel, plan, [own for _, own in key_sets], not old, last),
        out_shape,
        [query, *(rows for rows, _ in key_sets), *old],
        4 * total * count * width,
        12 * total * width,
        total * count,
        scratch=[pltpu.VMEM((2, total, LANES), F32)],
    )


def unpack_kernel(plan, place_ref, home_ref, out_ref):
    slot = column(place_ref[0:1, :])[:, 0:1]
    match = as_bf16(iota((plan.files, plan.total), 1) == slot)
    out_ref[...] = jnp.dot(match, home_ref[...], preferred_element_type=F32).astype(BF16)


def smooth(plan, embeddings, bucket):
    files, width, total = plan.files, plan.width, plan.total
    bucket = bucket.reshape(1, files)

    def pack(which, rows, after=()):
        return call(
            functools.partial(pack_kernel, plan),
            (
                jax.ShapeDtypeStruct((total, width), BF16),
                jax.ShapeDtypeStruct((8, files), I32),
            ),
            [which, rows],
            2 * total * files * width,
            6 * files * width,
            after=after,
        )

    other_bucket = swapped(bucket, plan.half_bit, plan)
    other_rows = swapped(embeddings, plan.half_bit, plan)
    payload, place = pack(bucket, embeddings, (other_bucket,))
    own = exchange(payload, plan)
    mate = swapped(own, plan.core_bit, plan)
    relayed, _ = pack(other_bucket, other_rows, (own,))
    half = exchange(relayed, plan)
    sums = attend(plan, own, [(own, True), (mate, False)])
    mate_half = swapped(half, plan.core_bit, plan)
    sums = attend(plan, own, [(half, False)], sums)
    smoothed = attend(plan, own, [(mate_half, False)], sums, last=True)
    flags = [
        rows.reshape(plan.cells, plan.slots, width)[:, -1, FACTS * LANES]
        for rows in (own, mate, half, mate_half)
    ]
    return exchange(smoothed, plan), place, jnp.max(jnp.concatenate(flags)) > 0


def unpack(plan, home, place):
    return call(
        functools.partial(unpack_kernel, plan),
        jax.ShapeDtypeStruct((plan.files, plan.width), BF16),
        [place, home],
        2 * plan.total * plan.files * plan.width,
        6 * plan.files * plan.width,
    )


def body(embeddings, bucket):
    nx, ny = lax.axis_size("hx"), lax.axis_size("hy")
    most = 4 * BPD * CAP // (nx * ny)
    short, full = (
        Plan(nx, ny, *embeddings.shape, slots)
        for slots in (max(2 * TILE, most * 7 // 8 // TILE * TILE), most + TILE)
    )
    home, place, over = smooth(short, embeddings, bucket)

    def again(home, place):
        home, place, _ = smooth(full, embeddings, bucket)
        return unpack(full, home, place)

    return lax.cond(over, again, functools.partial(unpack, short), home, place)


def solution(mesh):
    return jax.shard_map(
        body,
        mesh=mesh,
        in_specs=(P(("hx", "hy"), None), P(("hx", "hy"))),
        out_specs=P(("hx", "hy"), None),
        check_vma=False,
    )
```

```python
import functools
import math

import jax
import jax.numpy as jnp
from jax import lax
from jax.experimental import pallas as pl
from jax.experimental.pallas import tpu as pltpu
from jax.sharding import PartitionSpec as P

BPD = 2
CAP = 512
TILE = 16
FACTS = 4
LANES = 128

sharpness = 32.0
epsilon = 1e-06

AXES = ("hx", "hy")
VMEM = pl.BlockSpec(memory_space=pltpu.VMEM)
ANY = pl.BlockSpec(memory_space=pl.ANY)
F32, BF16, I32 = jnp.float32, jnp.bfloat16, jnp.int32


class Plan:
    def __init__(self, nx, ny, files, width, slots):
        self.nx, self.ny, self.files, self.width, self.slots = nx, ny, files, width, slots
        self.devices = nx * ny
        self.cells = self.devices // 4
        self.total = self.cells * slots
        self.known = min(slots, LANES)
        self.core_bit, self.half_bit = ny, ny // 2
        self.groups = [
            [(2 * u + core) * ny + half * (ny // 2) + v for u in range(nx // 2) for v in range(ny // 2)]
            for core in range(2)
            for half in range(2)
        ]


def swapped(value, bit, plan):
    return lax.ppermute(value, AXES, [(i, i ^ bit) for i in range(plan.devices)])


def exchange(value, plan):
    shape = (plan.cells, plan.slots, plan.width)
    return lax.all_to_all(
        value.reshape(shape), AXES, split_axis=0, concat_axis=0, tiled=True, axis_index_groups=plan.groups
    ).reshape(plan.total, plan.width)


def call(kernel, out_shape, args, flops, moved, exps=0, after=(), scratch=(), limit=12):
    return pl.pallas_call(
        kernel,
        out_shape=out_shape,
        in_specs=[VMEM] * len(args) + [ANY] * len(after),
        out_specs=jax.tree.map(lambda _: VMEM, out_shape),
        scratch_shapes=list(scratch),
        compiler_params=pltpu.CompilerParams(vmem_limit_bytes=limit * 1024 * 1024),
        cost_estimate=pl.CostEstimate(flops=flops, bytes_accessed=moved, transcendentals=exps),
    )(*args, *after)


def iota(shape, dim):
    return lax.broadcasted_iota(I32, shape, dim)


def column(row):
    return jnp.broadcast_to(row, (LANES, row.shape[1])).T


def rows_dot(left, right):
    return lax.dot_general(left, right, (((1,), (1,)), ((), ())), preferred_element_type=F32)


def as_bf16(mask):
    return mask.astype(F32).astype(BF16)


def pack_kernel(plan, bucket_ref, rows_ref, *refs):
    out_ref, place_ref = refs[-2:]
    nx, ny, files, slots, known = plan.nx, plan.ny, plan.files, plan.slots, plan.known
    bucket = bucket_ref[...]
    low_b = ny.bit_length() - 1
    a = bucket >> (low_b + 1)
    b = (bucket >> 1) & (ny - 1)
    c = bucket & 1
    cell = (a & (nx // 2 - 1)) * (ny // 2) + (b & (ny // 2 - 1))
    tag = (a >> (nx.bit_length() - 2)) * 4 + (b >> (low_b - 1)) * 2 + c + 1
    order = cell * files + iota((1, files), 1)
    before = column(order)[:, :1] < order
    same = column(cell)[:, :1] == cell
    index = jnp.sum((before & same).astype(I32), axis=0, keepdims=True)
    over = jnp.max(index, axis=1, keepdims=True) >= slots - 1
    slot = jnp.where(index < slots - 1, cell * slots + index, plan.total)
    place_ref[...] = jnp.broadcast_to(slot, place_ref.shape)

    rows = rows_ref[...]
    wide = rows.astype(F32)
    square = jnp.sum(wide * wide, axis=1, keepdims=True)
    square = jnp.broadcast_to(square, (files, LANES)).T[0:1, :]
    inv = 1.0 / jnp.sqrt(square * (1.0 / plan.width) + epsilon)
    high = inv.astype(BF16).astype(F32)
    middle = (inv - high).astype(BF16).astype(F32)
    low = inv - high - middle
    which = iota((TILE, files), 0)
    facts = jnp.where(
        which == 0,
        tag.astype(F32),
        jnp.where(which == 1, high, jnp.where(which == 2, middle, jnp.where(which == 3, low, 0.0))),
    ).astype(BF16)
    last = iota((TILE, known), 0) == TILE - 1
    flag = jnp.broadcast_to(over.astype(F32), (TILE, LANES))
    for block in range(plan.cells):
        match = as_bf16(iota((slots, files), 0) + block * slots == slot)
        packed = jnp.dot(match, rows, preferred_element_type=F32)
        here = block * slots
        out_ref[here : here + slots, :] = packed.astype(BF16)
        line = rows_dot(facts, match)
        tail = slice(here + slots - TILE, here + slots)
        for fact in range(FACTS):
            lanes = slice(fact * LANES, fact * LANES + known)
            out_ref[tail, lanes] = jnp.where(
                last, line[fact : fact + 1, :known], packed[slots - TILE :, lanes]
            ).astype(BF16)
        lanes = slice(FACTS * LANES, (FACTS + 1) * LANES)
        out_ref[tail, lanes] = jnp.where(
            iota((TILE, LANES), 0) == TILE - 1, flag, packed[slots - TILE :, lanes]
        ).astype(BF16)


def facts_of(plan, ref):
    slots, known = plan.slots, plan.known
    tags, invs, over = [], [], jnp.zeros((1, LANES), F32)
    for source in range(plan.cells):
        end = (source + 1) * slots
        lines = ref[end - TILE : end, 0 : (FACTS + 1) * LANES].astype(F32)[TILE - 1 : TILE, :]
        over = jnp.maximum(over, lines[:, FACTS * LANES :])
        tag, high, middle, low = (
            lines[:, fact * LANES : fact * LANES + known] for fact in range(FACTS)
        )
        tags.append(tag)
        invs.append(high + middle + low)
        if known < slots:
            empty = jnp.zeros((1, slots - known), F32)
            tags.append(empty)
            invs.append(empty)
    return jnp.concatenate(tags, axis=1), jnp.concatenate(invs, axis=1), over


def attend_kernel(plan, sets, first, last, *refs):
    refs = list(refs)
    query_ref = refs.pop(0)
    keys = [(refs.pop(0), own) for own in sets]
    if not first:
        old_over_ref, old_ref, old_sum_ref = refs[:3]
        del refs[:3]
    if last:
        over_ref, out_ref, column_ref = refs
    else:
        over_ref, out_ref, sum_ref, column_ref = refs
    total, width = plan.total, plan.width
    tag, inv, over = facts_of(plan, query_ref)
    if not first:
        over = jnp.maximum(over, old_over_ref[0:1, :])
    place = jnp.maximum(tag.astype(I32) - 1, 0)
    bits = (2 << place) | (2 << (place ^ 1)) | (2 << (place ^ 2)) | (2 << (place ^ 4))
    column_ref[0] = column(inv * (sharpness / width * math.log2(math.e)))
    column_ref[1] = column(bits.astype(F32))
    key_facts = []
    for key_ref, own in keys:
        key_tag, key_inv, key_over = facts_of(plan, key_ref)
        key_facts.append((1 << key_tag.astype(I32), key_inv))
        over = jnp.maximum(over, key_over)
    over_ref[...] = jnp.broadcast_to(over, over_ref.shape)
    chunk = total // 2
    for step in range(2):
        here = slice(step * chunk, (step + 1) * chunk)
        query = query_ref[here, :]
        query_inv = column_ref[0, here, :][:, 0:1]
        query_bits = column_ref[1, here, :][:, 0:1].astype(I32)
        if first:
            numerator = jnp.zeros((chunk, width), F32)
            denominator = jnp.ones((chunk, LANES), F32)
        else:
            numerator, denominator = old_ref[here, :], old_sum_ref[here, :]
        for (key_ref, own), (key_bit, key_inv) in zip(keys, key_facts):
            score = rows_dot(query, key_ref[...]) * query_inv * key_inv
            live = (query_bits & key_bit) != 0
            if own:
                live = live & (iota((chunk, total), 0) + step * chunk != iota((chunk, total), 1))
            kernel = jnp.where(live, jnp.exp2(score), 0.0)
            denominator = denominator + jnp.sum(kernel, axis=1, keepdims=True)
            numerator = numerator + jnp.dot(
                kernel.astype(BF16), key_ref[...], preferred_element_type=F32
            )
        if last:
            out_ref[here, :] = (numerator / denominator[:, 0:1]).astype(BF16)
        else:
            out_ref[here, :] = numerator
            sum_ref[here, :] = denominator


def attend(plan, query, key_sets, old=(), last=False, weight=1):
    total, width = plan.total, plan.width
    count = len(key_sets) * total
    flag = jax.ShapeDtypeStruct((8, LANES), F32)
    if last:
        out_shape = (flag, jax.ShapeDtypeStruct((total, width), BF16))
    else:
        out_shape = (
            flag,
            jax.ShapeDtypeStruct((total, width), F32),
            jax.ShapeDtypeStruct((total, LANES), F32),
        )
    return call(
        functools.partial(attend_kernel, plan, [own for _, own in key_sets], not old, last),
        out_shape,
        [query, *(rows for rows, _ in key_sets), *old],
        weight * 4 * total * count * width,
        12 * total * width,
        total * count,
        scratch=[pltpu.VMEM((2, total, LANES), F32)],
        limit=18,
    )


def unpack_kernel(plan, place_ref, home_ref, out_ref):
    slot = column(place_ref[0:1, :])[:, 0:1]
    match = as_bf16(iota((plan.files, plan.total), 1) == slot)
    out_ref[...] = jnp.dot(match, home_ref[...], preferred_element_type=F32).astype(BF16)


def smooth(plan, embeddings, bucket):
    files, width, total = plan.files, plan.width, plan.total
    bucket = bucket.reshape(1, files)

    def pack(which, rows, after=()):
        return call(
            functools.partial(pack_kernel, plan),
            (
                jax.ShapeDtypeStruct((total, width), BF16),
                jax.ShapeDtypeStruct((8, files), I32),
            ),
            [which, rows],
            2 * total * files * width,
            6 * files * width,
            after=after,
        )

    other_bucket = swapped(bucket, plan.half_bit, plan)
    other_rows = swapped(embeddings, plan.half_bit, plan)
    payload, place = pack(bucket, embeddings)
    own = exchange(payload, plan)
    mate = swapped(own, plan.core_bit, plan)
    relayed, _ = pack(other_bucket, other_rows, (own,))
    half = exchange(relayed, plan)
    sums = attend(plan, own, [(own, True), (mate, False)])
    mate_half = swapped(half, plan.core_bit, plan)
    sums = attend(plan, own, [(half, False)], sums, weight=40)
    over, smoothed = attend(plan, own, [(mate_half, False)], sums, last=True)
    return exchange(smoothed, plan), place, over[0, 0] > 0


def unpack(plan, home, place):
    return call(
        functools.partial(unpack_kernel, plan),
        jax.ShapeDtypeStruct((plan.files, plan.width), BF16),
        [place, home],
        2 * plan.total * plan.files * plan.width,
        6 * plan.files * plan.width,
    )


def body(embeddings, bucket):
    nx, ny = lax.axis_size("hx"), lax.axis_size("hy")
    most = 4 * BPD * CAP // (nx * ny)
    short, full = (
        Plan(nx, ny, *embeddings.shape, slots)
        for slots in (max(2 * TILE, most * 7 // 8 // TILE * TILE), most + TILE)
    )
    home, place, over = smooth(short, embeddings, bucket)

    def again(home, place):
        home, place, _ = smooth(full, embeddings, bucket)
        return unpack(full, home, place)

    return lax.cond(over, again, functools.partial(unpack, short), home, place)


def solution(mesh):
    return jax.shard_map(
        body,
        mesh=mesh,
        in_specs=(P(("hx", "hy"), None), P(("hx", "hy"))),
        out_specs=P(("hx", "hy"), None),
        check_vma=False,
    )
```

```python
import functools
import math

import jax
import jax.numpy as jnp
from jax import lax
from jax.experimental import pallas as pl
from jax.experimental.pallas import tpu as pltpu
from jax.sharding import PartitionSpec as P

BPD = 2
CAP = 512
TILE = 16
FACTS = 4
LANES = 128

sharpness = 32.0
epsilon = 1e-06

AXES = ("hx", "hy")
VMEM = pl.BlockSpec(memory_space=pltpu.VMEM)
ANY = pl.BlockSpec(memory_space=pl.ANY)
SMEM = pl.BlockSpec(memory_space=pltpu.SMEM)
F32, BF16, I32 = jnp.float32, jnp.bfloat16, jnp.int32


class Plan:
    def __init__(self, nx, ny, files, width, slots):
        self.nx, self.ny, self.files, self.width, self.slots = nx, ny, files, width, slots
        self.devices = nx * ny
        self.cells = self.devices // 4
        self.total = self.cells * slots
        self.known = min(slots, LANES)
        self.core_bit, self.half_bit = ny, ny // 2 + ny // 4
        self.groups = [
            [
                (2 * u + core) * ny + half * (ny // 2) + (v ^ half * (ny // 4))
                for u in range(nx // 2)
                for v in range(ny // 2)
            ]
            for core in range(2)
            for half in range(2)
        ]


def swapped(value, bit, plan):
    return lax.ppermute(value, AXES, [(i, i ^ bit) for i in range(plan.devices)])


def exchange(value, plan):
    shape = (plan.cells, plan.slots, plan.width)
    return lax.all_to_all(
        value.reshape(shape), AXES, split_axis=0, concat_axis=0, tiled=True, axis_index_groups=plan.groups
    ).reshape(plan.total, plan.width)


def call(kernel, out_shape, args, flops, moved, exps=0, after=(), scratch=(), limit=12, out_specs=None):
    return pl.pallas_call(
        kernel,
        out_shape=out_shape,
        in_specs=[VMEM] * len(args) + [ANY] * len(after),
        out_specs=out_specs or jax.tree.map(lambda _: VMEM, out_shape),
        scratch_shapes=list(scratch),
        compiler_params=pltpu.CompilerParams(vmem_limit_bytes=limit * 1024 * 1024),
        cost_estimate=pl.CostEstimate(flops=flops, bytes_accessed=moved, transcendentals=exps),
    )(*args, *after)


def iota(shape, dim):
    return lax.broadcasted_iota(I32, shape, dim)


def column(row):
    return jnp.broadcast_to(row, (LANES, row.shape[1])).T


def rows_dot(left, right):
    return lax.dot_general(left, right, (((1,), (1,)), ((), ())), preferred_element_type=F32)


def as_bf16(mask):
    return mask.astype(F32).astype(BF16)


def pack_kernel(plan, bucket_ref, rows_ref, *refs):
    out_ref, place_ref = refs[-2:]
    nx, ny, files, slots, known = plan.nx, plan.ny, plan.files, plan.slots, plan.known
    bucket = bucket_ref[...]
    low_b = ny.bit_length() - 1
    a = bucket >> (low_b + 1)
    b = (bucket >> 1) & (ny - 1)
    c = bucket & 1
    cell = (a & (nx // 2 - 1)) * (ny // 2) + (b & (ny // 2 - 1))
    tag = (a >> (nx.bit_length() - 2)) * 4 + (b >> (low_b - 1)) * 2 + c + 1
    order = cell * files + iota((1, files), 1)
    before = column(order)[:, :1] < order
    same = column(cell)[:, :1] == cell
    index = jnp.sum((before & same).astype(I32), axis=0, keepdims=True)
    over = jnp.max(index, axis=1, keepdims=True) >= slots - 1
    slot = jnp.where(index < slots - 1, cell * slots + index, plan.total)
    place_ref[...] = jnp.broadcast_to(slot, place_ref.shape)

    rows = rows_ref[...]
    wide = rows.astype(F32)
    square = jnp.sum(wide * wide, axis=1, keepdims=True)
    square = jnp.broadcast_to(square, (files, LANES)).T[0:1, :]
    inv = 1.0 / jnp.sqrt(square * (1.0 / plan.width) + epsilon)
    high = inv.astype(BF16).astype(F32)
    middle = (inv - high).astype(BF16).astype(F32)
    low = inv - high - middle
    which = iota((TILE, files), 0)
    facts = jnp.where(
        which == 0,
        tag.astype(F32),
        jnp.where(which == 1, high, jnp.where(which == 2, middle, jnp.where(which == 3, low, 0.0))),
    ).astype(BF16)
    match = as_bf16(iota((plan.total, files), 0) == slot)
    out_ref[...] = jnp.dot(match, rows, preferred_element_type=F32).astype(BF16)
    last = iota((TILE, LANES), 0) == TILE - 1
    flag = jnp.broadcast_to(over.astype(F32), (TILE, LANES))
    for block in range(plan.cells):
        here, end = block * slots, (block + 1) * slots
        line = rows_dot(facts, match[here:end, :])
        tail = slice(end - TILE, end)
        old = out_ref[tail, 0 : (FACTS + 1) * LANES].astype(F32)
        for fact in range(FACTS):
            lanes = slice(fact * LANES, fact * LANES + known)
            out_ref[tail, lanes] = jnp.where(
                last[:, :known], line[fact : fact + 1, :known], old[:, lanes]
            ).astype(BF16)
        lanes = slice(FACTS * LANES, (FACTS + 1) * LANES)
        out_ref[tail, lanes] = jnp.where(last, flag, old[:, lanes]).astype(BF16)


def facts_of(plan, ref):
    slots, known = plan.slots, plan.known
    tags, invs, over = [], [], jnp.zeros((1, LANES), F32)
    for source in range(plan.cells):
        end = (source + 1) * slots
        lines = ref[end - TILE : end, 0 : (FACTS + 1) * LANES].astype(F32)[TILE - 1 : TILE, :]
        over = jnp.maximum(over, lines[:, FACTS * LANES :])
        tag, high, middle, low = (
            lines[:, fact * LANES : fact * LANES + known] for fact in range(FACTS)
        )
        tags.append(tag)
        invs.append(high + middle + low)
        if known < slots:
            empty = jnp.zeros((1, slots - known), F32)
            tags.append(empty)
            invs.append(empty)
    return jnp.concatenate(tags, axis=1), jnp.concatenate(invs, axis=1), over


def attend_kernel(plan, sets, olds, *refs):
    refs = list(refs)
    query_ref = refs.pop(0)
    keys = [(refs.pop(0), own) for own in sets]
    old_refs = refs[: 2 * olds]
    over_ref, out_ref, column_ref = refs[2 * olds :]
    total, width = plan.total, plan.width
    chunk = total // 2
    tag, inv, over = facts_of(plan, query_ref)
    for old_over_ref in old_refs[0::2]:
        over = jnp.maximum(over, old_over_ref[0:1, :])
    place = jnp.maximum(tag.astype(I32) - 1, 0)
    bits = (2 << place) | (2 << (place ^ 1)) | (2 << (place ^ 2)) | (2 << (place ^ 4))
    bits = jnp.where(tag > 0.0, bits, 0)
    column_ref[0] = column(inv * (sharpness / width * math.log2(math.e)))
    column_ref[1] = column(bits.astype(F32))
    key_facts = []
    for key_ref, own in keys:
        key_tag, key_inv, key_over = facts_of(plan, key_ref)
        key_facts.append((1 << key_tag.astype(I32), key_inv))
        over = jnp.maximum(over, key_over)
    if olds:
        over_ref[0] = jnp.max(over).astype(I32)
    else:
        over_ref[...] = jnp.broadcast_to(over, over_ref.shape)
    for step in range(2):
        here = slice(step * chunk, (step + 1) * chunk)
        query = query_ref[here, :]
        query_inv = column_ref[0, here, :][:, 0:1]
        query_bits = column_ref[1, here, :][:, 0:1].astype(I32)
        numerator, denominator = 0.0, 0.0
        for (key_ref, own), (key_bit, key_inv) in zip(keys, key_facts):
            score = rows_dot(query, key_ref[...]) * query_inv * key_inv
            live = (query_bits & key_bit) != 0
            if own:
                live = live & (iota((chunk, total), 0) + step * chunk != iota((chunk, total), 1))
            kernel = jnp.where(live, jnp.exp2(score), 0.0)
            denominator = denominator + jnp.sum(kernel, axis=1, keepdims=True)
            numerator = numerator + jnp.dot(
                kernel.astype(BF16), key_ref[...], preferred_element_type=F32
            )
        for old_ref in old_refs[1::2]:
            numerator = numerator + old_ref[here, 0:width]
            denominator = denominator + old_ref[here, width:][:, 0:1]
        if olds:
            out_ref[here, :] = (numerator / (1.0 + denominator)).astype(BF16)
        else:
            out_ref[here, 0:width] = numerator
            out_ref[here, width:] = jnp.broadcast_to(denominator, (chunk, LANES))


def attend(plan, query, key_sets, olds=(), weight=1):
    total, width = plan.total, plan.width
    count = len(key_sets) * total
    return call(
        functools.partial(attend_kernel, plan, [own for _, own in key_sets], len(olds)),
        (
            jax.ShapeDtypeStruct((1,), I32) if olds else jax.ShapeDtypeStruct((8, LANES), F32),
            jax.ShapeDtypeStruct((total, width), BF16)
            if olds
            else jax.ShapeDtypeStruct((total, width + LANES), F32),
        ),
        [query, *(rows for rows, _ in key_sets), *(part for old in olds for part in old)],
        weight * 4 * total * count * width,
        12 * total * width,
        total * count,
        scratch=[pltpu.VMEM((2, total, LANES), F32)],
        limit=26,
        out_specs=(SMEM if olds else VMEM, VMEM),
    )


def unpack_kernel(plan, place_ref, home_ref, out_ref):
    slot = column(place_ref[0:1, :])[:, 0:1]
    match = as_bf16(iota((plan.files, plan.total), 1) == slot)
    out_ref[...] = jnp.dot(match, home_ref[...], preferred_element_type=F32).astype(BF16)


def smooth(plan, embeddings, bucket):
    files, width, total = plan.files, plan.width, plan.total
    bucket = bucket.reshape(1, files)

    def pack(which, rows, after=()):
        return call(
            functools.partial(pack_kernel, plan),
            (
                jax.ShapeDtypeStruct((total, width), BF16),
                jax.ShapeDtypeStruct((8, files), I32),
            ),
            [which, rows],
            2 * total * files * width,
            6 * files * width,
            after=after,
        )

    other_bucket = swapped(bucket, plan.half_bit, plan)
    other_rows = swapped(embeddings, plan.half_bit, plan)
    payload, place = pack(bucket, embeddings)
    own = lax.cond(
        lax.axis_index(AXES) != plan.devices, lambda payload: exchange(payload, plan), lambda payload: payload, payload
    )
    mate = swapped(own, plan.core_bit, plan)
    relayed, _ = pack(other_bucket, other_rows, (own,))
    half = exchange(relayed, plan)
    near = attend(plan, own, [(own, True), (mate, False)])
    mate_half = swapped(half, plan.core_bit, plan)
    far = attend(plan, own, [(half, False)], weight=40)
    over, smoothed = attend(plan, own, [(mate_half, False)], [near, far])
    return smoothed, place, over[0] > 0


def unpack(plan, smoothed, place):
    home = exchange(smoothed, plan)
    return call(
        functools.partial(unpack_kernel, plan),
        jax.ShapeDtypeStruct((plan.files, plan.width), BF16),
        [place, home],
        2 * plan.total * plan.files * plan.width,
        6 * plan.files * plan.width,
    )


def body(embeddings, bucket):
    nx, ny = lax.axis_size("hx"), lax.axis_size("hy")
    most = 4 * BPD * CAP // (nx * ny)
    short, full = (
        Plan(nx, ny, *embeddings.shape, slots)
        for slots in (max(2 * TILE, most * 7 // 8 // TILE * TILE), most + TILE)
    )
    smoothed, place, over = smooth(short, embeddings, bucket)

    def again(smoothed, place):
        smoothed, place, _ = smooth(full, embeddings, bucket)
        return unpack(full, smoothed, place)

    return lax.cond(over, again, functools.partial(unpack, short), smoothed, place)


def solution(mesh):
    return jax.shard_map(
        body,
        mesh=mesh,
        in_specs=(P(("hx", "hy"), None), P(("hx", "hy"))),
        out_specs=P(("hx", "hy"), None),
        check_vma=False,
    )
```

```python
import functools
import math

import jax
import jax.numpy as jnp
from jax import lax
from jax.experimental import pallas as pl
from jax.experimental.pallas import tpu as pltpu
from jax.sharding import PartitionSpec as P

BPD = 2
CAP = 512
TILE = 16
FACTS = 4
LANES = 128

sharpness = 32.0
epsilon = 1e-06

AXES = ("hx", "hy")
VMEM = pl.BlockSpec(memory_space=pltpu.VMEM)
ANY = pl.BlockSpec(memory_space=pl.ANY)
SMEM = pl.BlockSpec(memory_space=pltpu.SMEM)
F32, BF16, I32 = jnp.float32, jnp.bfloat16, jnp.int32


class Plan:
    def __init__(self, nx, ny, files, width, slots):
        self.nx, self.ny, self.files, self.width, self.slots = nx, ny, files, width, slots
        self.devices = nx * ny
        self.cells = self.devices // 4
        self.total = self.cells * slots
        self.known = min(slots, LANES)
        self.core_bit, self.half_bit = ny, ny // 2 + ny // 4
        self.groups = [
            turned(
                [
                    (2 * u + core) * ny + half * (ny // 2) + (v ^ half * (ny // 4))
                    for u in range(nx // 2)
                    for v in range(ny // 2)
                ]
            )
            for core in range(2)
            for half in range(2)
        ]


def turned(members):
    return [members[-1 - i // 2 if i % 2 else i // 2] for i in range(len(members))]


def swapped(value, bit, plan):
    return lax.ppermute(value, AXES, [(i, i ^ bit) for i in range(plan.devices)])


def exchange(value, plan):
    shape = (plan.cells, plan.slots, plan.width)
    return lax.all_to_all(
        value.reshape(shape), AXES, split_axis=0, concat_axis=0, tiled=True, axis_index_groups=plan.groups
    ).reshape(plan.total, plan.width)


def call(kernel, out_shape, args, flops, moved, exps=0, after=(), scratch=(), limit=12, out_specs=None):
    return pl.pallas_call(
        kernel,
        out_shape=out_shape,
        in_specs=[VMEM] * len(args) + [ANY] * len(after),
        out_specs=out_specs or jax.tree.map(lambda _: VMEM, out_shape),
        scratch_shapes=list(scratch),
        compiler_params=pltpu.CompilerParams(vmem_limit_bytes=limit * 1024 * 1024),
        cost_estimate=pl.CostEstimate(flops=flops, bytes_accessed=moved, transcendentals=exps),
    )(*args, *after)


def iota(shape, dim):
    return lax.broadcasted_iota(I32, shape, dim)


def column(row):
    return jnp.broadcast_to(row, (LANES, row.shape[1])).T


def rows_dot(left, right):
    return lax.dot_general(left, right, (((1,), (1,)), ((), ())), preferred_element_type=F32)


def as_bf16(mask):
    return mask.astype(F32).astype(BF16)


def place_kernel(plan, bucket_ref, rows_ref, place_ref):
    nx, ny, files, slots = plan.nx, plan.ny, plan.files, plan.slots
    bucket = bucket_ref[...]
    low_b = ny.bit_length() - 1
    a = bucket >> (low_b + 1)
    b = (bucket >> 1) & (ny - 1)
    c = bucket & 1
    cell = (a & (nx // 2 - 1)) * (ny // 2) + (b & (ny // 2 - 1))
    tag = (a >> (nx.bit_length() - 2)) * 4 + (b >> (low_b - 1)) * 2 + c + 1
    order = cell * files + iota((1, files), 1)
    before = column(order)[:, :1] < order
    same = column(cell)[:, :1] == cell
    index = jnp.sum((before & same).astype(I32), axis=0, keepdims=True)
    over = (jnp.max(index, axis=1, keepdims=True) >= slots - 1).astype(F32)
    slot = jnp.where(index < slots - 1, cell * slots + index, plan.total)
    wide = rows_ref[...].astype(F32)
    square = jnp.sum(wide * wide, axis=1, keepdims=True)
    square = jnp.broadcast_to(square, (files, LANES)).T[0:1, :]
    inv = 1.0 / jnp.sqrt(square * (1.0 / plan.width) + epsilon)
    high = inv.astype(BF16).astype(F32)
    middle = (inv - high).astype(BF16).astype(F32)
    low = inv - high - middle
    line = iota((8, files), 0)
    place = jnp.zeros((8, files), F32)
    for index, value in enumerate((tag.astype(F32), high, middle, low, over, slot.astype(F32))):
        place = jnp.where(line == index, value, place)
    place_ref[...] = place


def pack_kernel(plan, place_ref, rows_ref, *refs):
    out_ref = refs[-1]
    files, slots, known = plan.files, plan.slots, plan.known
    place = place_ref[...]
    facts = jnp.concatenate([place, jnp.zeros((TILE - 8, files), F32)], axis=0)
    facts = jnp.where(iota((TILE, files), 0) < FACTS, facts, 0.0).astype(BF16)
    over, slot = place[4:5, 0:LANES], place[5:6, :].astype(I32)
    rows = rows_ref[...]
    match = as_bf16(iota((plan.total, files), 0) == slot)
    out_ref[...] = jnp.dot(match, rows, preferred_element_type=F32).astype(BF16)
    last = iota((TILE, LANES), 0) == TILE - 1
    flag = jnp.broadcast_to(over, (TILE, LANES))
    for block in range(plan.cells):
        here, end = block * slots, (block + 1) * slots
        line = rows_dot(facts, match[here:end, :])
        tail = slice(end - TILE, end)
        old = out_ref[tail, 0 : (FACTS + 1) * LANES].astype(F32)
        for fact in range(FACTS):
            lanes = slice(fact * LANES, fact * LANES + known)
            out_ref[tail, lanes] = jnp.where(
                last[:, :known], line[fact : fact + 1, :known], old[:, lanes]
            ).astype(BF16)
        lanes = slice(FACTS * LANES, (FACTS + 1) * LANES)
        out_ref[tail, lanes] = jnp.where(last, flag, old[:, lanes]).astype(BF16)


def facts_of(plan, ref):
    slots, known = plan.slots, plan.known
    tags, invs, over = [], [], jnp.zeros((1, LANES), F32)
    for source in range(plan.cells):
        end = (source + 1) * slots
        lines = ref[end - TILE : end, 0 : (FACTS + 1) * LANES].astype(F32)[TILE - 1 : TILE, :]
        over = jnp.maximum(over, lines[:, FACTS * LANES :])
        tag, high, middle, low = (
            lines[:, fact * LANES : fact * LANES + known] for fact in range(FACTS)
        )
        tags.append(tag)
        invs.append(high + middle + low)
        if known < slots:
            empty = jnp.zeros((1, slots - known), F32)
            tags.append(empty)
            invs.append(empty)
    return jnp.concatenate(tags, axis=1), jnp.concatenate(invs, axis=1), over


def attend_kernel(plan, sets, olds, *refs):
    refs = list(refs)
    query_ref = refs.pop(0)
    keys = [(refs.pop(0), own) for own in sets]
    old_refs = refs[: 2 * olds]
    over_ref, out_ref, column_ref = refs[2 * olds :]
    total, width = plan.total, plan.width
    chunk = total // 2
    tag, inv, over = facts_of(plan, query_ref)
    for old_over_ref in old_refs[0::2]:
        over = jnp.maximum(over, old_over_ref[0:1, :])
    place = jnp.maximum(tag.astype(I32) - 1, 0)
    bits = (2 << place) | (2 << (place ^ 1)) | (2 << (place ^ 2)) | (2 << (place ^ 4))
    bits = jnp.where(tag > 0.0, bits, 0)
    column_ref[0] = column(inv * (sharpness / width * math.log2(math.e)))
    column_ref[1] = column(bits.astype(F32))
    key_facts = []
    for key_ref, own in keys:
        key_tag, key_inv, key_over = facts_of(plan, key_ref)
        key_facts.append((1 << key_tag.astype(I32), key_inv))
        over = jnp.maximum(over, key_over)
    if olds:
        over_ref[0] = jnp.max(over).astype(I32)
    else:
        over_ref[...] = jnp.broadcast_to(over, over_ref.shape)
    for step in range(2):
        here = slice(step * chunk, (step + 1) * chunk)
        query = query_ref[here, :]
        query_inv = column_ref[0, here, :][:, 0:1]
        query_bits = column_ref[1, here, :][:, 0:1].astype(I32)
        numerator, denominator = 0.0, 0.0
        for (key_ref, own), (key_bit, key_inv) in zip(keys, key_facts):
            score = rows_dot(query, key_ref[...]) * query_inv * key_inv
            live = (query_bits & key_bit) != 0
            if own:
                live = live & (iota((chunk, total), 0) + step * chunk != iota((chunk, total), 1))
            kernel = jnp.where(live, jnp.exp2(score), 0.0)
            denominator = denominator + jnp.sum(kernel, axis=1, keepdims=True)
            numerator = numerator + jnp.dot(
                kernel.astype(BF16), key_ref[...], preferred_element_type=F32
            )
        for old_ref in old_refs[1::2]:
            numerator = numerator + old_ref[here, 0:width]
            denominator = denominator + old_ref[here, width:][:, 0:1]
        if olds:
            out_ref[here, :] = (numerator / (1.0 + denominator)).astype(BF16)
        else:
            out_ref[here, 0:width] = numerator
            out_ref[here, width:] = jnp.broadcast_to(denominator, (chunk, LANES))


def attend(plan, query, key_sets, olds=(), weight=1):
    total, width = plan.total, plan.width
    count = len(key_sets) * total
    return call(
        functools.partial(attend_kernel, plan, [own for _, own in key_sets], len(olds)),
        (
            jax.ShapeDtypeStruct((1,), I32) if olds else jax.ShapeDtypeStruct((8, LANES), F32),
            jax.ShapeDtypeStruct((total, width), BF16)
            if olds
            else jax.ShapeDtypeStruct((total, width + LANES), F32),
        ),
        [query, *(rows for rows, _ in key_sets), *(part for old in olds for part in old)],
        weight * 4 * total * count * width,
        12 * total * width,
        total * count,
        scratch=[pltpu.VMEM((2, total, LANES), F32)],
        limit=26,
        out_specs=(SMEM if olds else VMEM, VMEM),
    )


def unpack_kernel(plan, place_ref, home_ref, out_ref):
    slot = column(place_ref[5:6, :])[:, 0:1].astype(I32)
    match = as_bf16(iota((plan.files, plan.total), 1) == slot)
    out_ref[...] = jnp.dot(match, home_ref[...], preferred_element_type=F32).astype(BF16)


def smooth(plan, embeddings, bucket):
    files, width, total = plan.files, plan.width, plan.total
    bucket = bucket.reshape(1, files)

    def pack(place, rows, after=()):
        return call(
            functools.partial(pack_kernel, plan),
            jax.ShapeDtypeStruct((total, width), BF16),
            [place, rows],
            2 * total * files * width,
            6 * files * width,
            after=after,
        )

    other_rows = swapped(embeddings, plan.half_bit, plan)
    place = call(
        functools.partial(place_kernel, plan),
        jax.ShapeDtypeStruct((8, files), F32),
        [bucket, embeddings],
        4 * files * files,
        2 * files * width,
    )
    other_place = swapped(place, plan.half_bit, plan)
    payload = pack(place, embeddings)
    own = lax.cond(
        lax.axis_index(AXES) != plan.devices, lambda payload: exchange(payload, plan), lambda payload: payload, payload
    )
    mate = swapped(own, plan.core_bit, plan)
    relayed = pack(other_place, other_rows, (own,))
    half = exchange(relayed, plan)
    near = attend(plan, own, [(own, True), (mate, False)])
    mate_half = swapped(half, plan.core_bit, plan)
    far = attend(plan, own, [(half, False)], weight=40)
    over, smoothed = attend(plan, own, [(mate_half, False)], [near, far])
    return smoothed, place, over[0] > 0


def unpack(plan, smoothed, place):
    home = exchange(smoothed, plan)
    return call(
        functools.partial(unpack_kernel, plan),
        jax.ShapeDtypeStruct((plan.files, plan.width), BF16),
        [place, home],
        2 * plan.total * plan.files * plan.width,
        6 * plan.files * plan.width,
    )


def body(embeddings, bucket):
    nx, ny = lax.axis_size("hx"), lax.axis_size("hy")
    most = 4 * BPD * CAP // (nx * ny)
    short, full = (
        Plan(nx, ny, *embeddings.shape, slots)
        for slots in (max(2 * TILE, most * 7 // 8 // TILE * TILE), most + TILE)
    )
    smoothed, place, over = smooth(short, embeddings, bucket)

    def again(smoothed, place):
        smoothed, place, _ = smooth(full, embeddings, bucket)
        return unpack(full, smoothed, place)

    return lax.cond(over, again, functools.partial(unpack, short), smoothed, place)


def solution(mesh):
    return jax.shard_map(
        body,
        mesh=mesh,
        in_specs=(P(("hx", "hy"), None), P(("hx", "hy"))),
        out_specs=P(("hx", "hy"), None),
        check_vma=False,
    )
```

```python
import functools
import math

import jax
import jax.numpy as jnp
from jax import lax
from jax.experimental import pallas as pl
from jax.experimental.pallas import tpu as pltpu
from jax.sharding import PartitionSpec as P

BPD = 2
CAP = 512
TILE = 16
FACTS = 4
LANES = 128

sharpness = 32.0
epsilon = 1e-06

AXES = ("hx", "hy")
VMEM = pl.BlockSpec(memory_space=pltpu.VMEM)
ANY = pl.BlockSpec(memory_space=pl.ANY)
SMEM = pl.BlockSpec(memory_space=pltpu.SMEM)
F32, BF16, I32 = jnp.float32, jnp.bfloat16, jnp.int32


class Plan:
    def __init__(self, nx, ny, files, width, slots):
        self.nx, self.ny, self.files, self.width, self.slots = nx, ny, files, width, slots
        self.devices = nx * ny
        self.cells = self.devices // 4
        self.total = self.cells * slots
        self.known = min(slots, LANES)
        self.core_bit, self.half_bit = ny, ny // 2 + ny // 4
        self.groups = [
            turned(
                [
                    (2 * u + core) * ny + half * (ny // 2) + (v ^ half * (ny // 4))
                    for u in range(nx // 2)
                    for v in range(ny // 2)
                ]
            )
            for core in range(2)
            for half in range(2)
        ]


def turned(members):
    return [members[-1 - i // 2 if i % 2 else i // 2] for i in range(len(members))]


def swapped(value, bit, plan):
    return lax.ppermute(value, AXES, [(i, i ^ bit) for i in range(plan.devices)])


def exchange(value, plan):
    shape = (plan.cells, plan.slots, plan.width)
    return lax.all_to_all(
        value.reshape(shape), AXES, split_axis=0, concat_axis=0, tiled=True, axis_index_groups=plan.groups
    ).reshape(plan.total, plan.width)


def call(kernel, out_shape, args, flops, moved, exps=0, after=(), scratch=(), limit=12, out_specs=None):
    return pl.pallas_call(
        kernel,
        out_shape=out_shape,
        in_specs=[VMEM] * len(args) + [ANY] * len(after),
        out_specs=out_specs or jax.tree.map(lambda _: VMEM, out_shape),
        scratch_shapes=list(scratch),
        compiler_params=pltpu.CompilerParams(vmem_limit_bytes=limit * 1024 * 1024),
        cost_estimate=pl.CostEstimate(flops=flops, bytes_accessed=moved, transcendentals=exps),
    )(*args, *after)


def iota(shape, dim):
    return lax.broadcasted_iota(I32, shape, dim)


def column(row):
    return jnp.broadcast_to(row, (LANES, row.shape[1])).T


def rows_dot(left, right):
    return lax.dot_general(left, right, (((1,), (1,)), ((), ())), preferred_element_type=F32)


def as_bf16(mask):
    return mask.astype(F32).astype(BF16)


def place_kernel(plan, bucket_ref, rows_ref, place_ref):
    nx, ny, files, slots = plan.nx, plan.ny, plan.files, plan.slots
    bucket = bucket_ref[...]
    low_b = ny.bit_length() - 1
    a = bucket >> (low_b + 1)
    b = (bucket >> 1) & (ny - 1)
    c = bucket & 1
    cell = (a & (nx // 2 - 1)) * (ny // 2) + (b & (ny // 2 - 1))
    tag = (a >> (nx.bit_length() - 2)) * 4 + (b >> (low_b - 1)) * 2 + c + 1
    order = cell * files + iota((1, files), 1)
    before = column(order)[:, :1] < order
    same = column(cell)[:, :1] == cell
    index = jnp.sum((before & same).astype(I32), axis=0, keepdims=True)
    over = (jnp.max(index, axis=1, keepdims=True) >= slots - 1).astype(F32)
    slot = jnp.where(index < slots - 1, cell * slots + index, plan.total)
    wide = rows_ref[...].astype(F32)
    square = jnp.sum(wide * wide, axis=1, keepdims=True)
    square = jnp.broadcast_to(square, (files, LANES)).T[0:1, :]
    inv = 1.0 / jnp.sqrt(square * (1.0 / plan.width) + epsilon)
    high = inv.astype(BF16).astype(F32)
    middle = (inv - high).astype(BF16).astype(F32)
    low = inv - high - middle
    line = iota((8, files), 0)
    place = jnp.zeros((8, files), F32)
    for index, value in enumerate((tag.astype(F32), high, middle, low, over, slot.astype(F32))):
        place = jnp.where(line == index, value, place)
    place_ref[...] = place


def pack_kernel(plan, place_ref, rows_ref, out_ref, info_ref):
    files, slots, known = plan.files, plan.slots, plan.known
    place = place_ref[...]
    facts = jnp.concatenate([place, jnp.zeros((TILE - 8, files), F32)], axis=0)
    facts = jnp.where(iota((TILE, files), 0) < FACTS, facts, 0.0).astype(BF16)
    over, slot = place[4:5, 0:LANES], place[5:6, :].astype(I32)
    match = as_bf16(iota((plan.total, files), 0) == slot)
    out_ref[...] = jnp.dot(match, rows_ref[...], preferred_element_type=F32).astype(BF16)
    info_ref[...] = jnp.zeros(info_ref.shape, F32)
    info_ref[0:8, 0:files] = place
    for block in range(plan.cells):
        line = rows_dot(facts, match[block * slots : (block + 1) * slots, :])
        row = slice(8 + block, 9 + block)
        for fact in range(FACTS):
            info_ref[row, fact * LANES : fact * LANES + known] = line[fact : fact + 1, :known]
        info_ref[row, FACTS * LANES : (FACTS + 1) * LANES] = over
    add_facts(plan, info_ref, out_ref)


def add_facts(plan, info_ref, out_ref):
    size = (FACTS + 1) * LANES
    last = iota((TILE, size), 0) == TILE - 1
    for block in range(plan.cells):
        end = (block + 1) * plan.slots
        tail = slice(end - TILE, end)
        out_ref[tail, 0:size] = jnp.where(
            last, info_ref[8 + block : 9 + block, 0:size], out_ref[tail, 0:size].astype(F32)
        ).astype(BF16)


def relay_kernel(plan, info_ref, rows_ref, after_ref, out_ref):
    del after_ref
    slot = info_ref[5:6, 0 : plan.files].astype(I32)
    match = as_bf16(iota((plan.total, plan.files), 0) == slot)
    out_ref[...] = jnp.dot(match, rows_ref[...], preferred_element_type=F32).astype(BF16)
    add_facts(plan, info_ref, out_ref)


def facts_of(plan, ref):
    slots, known = plan.slots, plan.known
    tags, invs, over = [], [], jnp.zeros((1, LANES), F32)
    for source in range(plan.cells):
        end = (source + 1) * slots
        lines = ref[end - TILE : end, 0 : (FACTS + 1) * LANES].astype(F32)[TILE - 1 : TILE, :]
        over = jnp.maximum(over, lines[:, FACTS * LANES :])
        tag, high, middle, low = (
            lines[:, fact * LANES : fact * LANES + known] for fact in range(FACTS)
        )
        tags.append(tag)
        invs.append(high + middle + low)
        if known < slots:
            empty = jnp.zeros((1, slots - known), F32)
            tags.append(empty)
            invs.append(empty)
    return jnp.concatenate(tags, axis=1), jnp.concatenate(invs, axis=1), over


def attend_kernel(plan, sets, olds, *refs):
    refs = list(refs)
    query_ref = refs.pop(0)
    keys = [(refs.pop(0), own) for own in sets]
    old_refs = refs[: 2 * olds]
    over_ref, out_ref, column_ref = refs[2 * olds :]
    total, width = plan.total, plan.width
    chunk = total // 2
    tag, inv, over = facts_of(plan, query_ref)
    for old_over_ref in old_refs[0::2]:
        over = jnp.maximum(over, old_over_ref[0:1, :])
    place = jnp.maximum(tag.astype(I32) - 1, 0)
    bits = (2 << place) | (2 << (place ^ 1)) | (2 << (place ^ 2)) | (2 << (place ^ 4))
    bits = jnp.where(tag > 0.0, bits, 0)
    column_ref[0] = column(inv * (sharpness / width * math.log2(math.e)))
    column_ref[1] = column(bits.astype(F32))
    key_facts = []
    for key_ref, own in keys:
        key_tag, key_inv, key_over = facts_of(plan, key_ref)
        key_facts.append((1 << key_tag.astype(I32), key_inv))
        over = jnp.maximum(over, key_over)
    if olds:
        over_ref[0] = jnp.max(over).astype(I32)
    else:
        over_ref[...] = jnp.broadcast_to(over, over_ref.shape)
    for step in range(2):
        here = slice(step * chunk, (step + 1) * chunk)
        query = query_ref[here, :]
        query_inv = column_ref[0, here, :][:, 0:1]
        query_bits = column_ref[1, here, :][:, 0:1].astype(I32)
        numerator, denominator = 0.0, 0.0
        for (key_ref, own), (key_bit, key_inv) in zip(keys, key_facts):
            score = rows_dot(query, key_ref[...]) * query_inv * key_inv
            live = (query_bits & key_bit) != 0
            if own:
                live = live & (iota((chunk, total), 0) + step * chunk != iota((chunk, total), 1))
            kernel = jnp.where(live, jnp.exp2(score), 0.0)
            denominator = denominator + jnp.sum(kernel, axis=1, keepdims=True)
            numerator = numerator + jnp.dot(
                kernel.astype(BF16), key_ref[...], preferred_element_type=F32
            )
        for old_ref in old_refs[1::2]:
            numerator = numerator + old_ref[here, 0:width]
            denominator = denominator + old_ref[here, width:][:, 0:1]
        if olds:
            out_ref[here, :] = (numerator / (1.0 + denominator)).astype(BF16)
        else:
            out_ref[here, 0:width] = numerator
            out_ref[here, width:] = jnp.broadcast_to(denominator, (chunk, LANES))


def attend(plan, query, key_sets, olds=(), weight=1):
    total, width = plan.total, plan.width
    count = len(key_sets) * total
    return call(
        functools.partial(attend_kernel, plan, [own for _, own in key_sets], len(olds)),
        (
            jax.ShapeDtypeStruct((1,), I32) if olds else jax.ShapeDtypeStruct((8, LANES), F32),
            jax.ShapeDtypeStruct((total, width), BF16)
            if olds
            else jax.ShapeDtypeStruct((total, width + LANES), F32),
        ),
        [query, *(rows for rows, _ in key_sets), *(part for old in olds for part in old)],
        weight * 4 * total * count * width,
        12 * total * width,
        total * count,
        scratch=[pltpu.VMEM((2, total, LANES), F32)],
        limit=26,
        out_specs=(SMEM if olds else VMEM, VMEM),
    )


def unpack_kernel(plan, place_ref, home_ref, out_ref):
    slot = column(place_ref[5:6, :])[:, 0:1].astype(I32)
    match = as_bf16(iota((plan.files, plan.total), 1) == slot)
    out_ref[...] = jnp.dot(match, home_ref[...], preferred_element_type=F32).astype(BF16)


def smooth(plan, embeddings, bucket):
    files, width, total = plan.files, plan.width, plan.total
    bucket = bucket.reshape(1, files)

    other_rows = swapped(embeddings, plan.half_bit, plan)
    place = call(
        functools.partial(place_kernel, plan),
        jax.ShapeDtypeStruct((8, files), F32),
        [bucket, embeddings],
        4 * files * files,
        2 * files * width,
    )
    payload, info = call(
        functools.partial(pack_kernel, plan),
        (
            jax.ShapeDtypeStruct((total, width), BF16),
            jax.ShapeDtypeStruct((8 + plan.cells, width), F32),
        ),
        [place, embeddings],
        2 * total * files * width,
        6 * files * width,
    )
    other_info = swapped(info, plan.half_bit, plan)
    own = lax.cond(
        lax.axis_index(AXES) != plan.devices, lambda payload: exchange(payload, plan), lambda payload: payload, payload
    )
    mate = swapped(own, plan.core_bit, plan)
    relayed = call(
        functools.partial(relay_kernel, plan),
        jax.ShapeDtypeStruct((total, width), BF16),
        [other_info, other_rows],
        2 * total * files * width,
        6 * files * width,
        after=(own,),
    )
    half = exchange(relayed, plan)
    near = attend(plan, own, [(own, True), (mate, False)])
    mate_half = swapped(half, plan.core_bit, plan)
    far = attend(plan, own, [(half, False)], weight=40)
    over, smoothed = attend(plan, own, [(mate_half, False)], [near, far])
    return smoothed, place, over[0] > 0


def unpack(plan, smoothed, place):
    home = exchange(smoothed, plan)
    return call(
        functools.partial(unpack_kernel, plan),
        jax.ShapeDtypeStruct((plan.files, plan.width), BF16),
        [place, home],
        2 * plan.total * plan.files * plan.width,
        6 * plan.files * plan.width,
    )


def body(embeddings, bucket):
    nx, ny = lax.axis_size("hx"), lax.axis_size("hy")
    most = 4 * BPD * CAP // (nx * ny)
    short, full = (
        Plan(nx, ny, *embeddings.shape, slots)
        for slots in (max(2 * TILE, most * 7 // 8 // TILE * TILE), most + TILE)
    )
    smoothed, place, over = smooth(short, embeddings, bucket)

    def again(smoothed, place):
        smoothed, place, _ = smooth(full, embeddings, bucket)
        return unpack(full, smoothed, place)

    return lax.cond(over, again, functools.partial(unpack, short), smoothed, place)


def solution(mesh):
    return jax.shard_map(
        body,
        mesh=mesh,
        in_specs=(P(("hx", "hy"), None), P(("hx", "hy"))),
        out_specs=P(("hx", "hy"), None),
        check_vma=False,
    )
```

```python
import functools
import math

import jax
import jax.numpy as jnp
from jax import lax
from jax.experimental import pallas as pl
from jax.experimental.pallas import tpu as pltpu
from jax.sharding import PartitionSpec as P

BPD = 2
CAP = 512
TILE = 16
FACTS = 4
LANES = 128

sharpness = 32.0
epsilon = 1e-06

AXES = ("hx", "hy")
VMEM = pl.BlockSpec(memory_space=pltpu.VMEM)
ANY = pl.BlockSpec(memory_space=pl.ANY)
SMEM = pl.BlockSpec(memory_space=pltpu.SMEM)
F32, BF16, I32 = jnp.float32, jnp.bfloat16, jnp.int32


class Plan:
    def __init__(self, nx, ny, files, width, slots):
        self.nx, self.ny, self.files, self.width, self.slots = nx, ny, files, width, slots
        self.devices = nx * ny
        self.cells = self.devices // 4
        self.total = self.cells * slots
        self.known = min(slots, LANES)
        self.core_bit, self.half_bit = ny, ny // 2 + ny // 4
        self.groups = [
            turned(
                [
                    (2 * u + core) * ny + half * (ny // 2) + (v ^ half * (ny // 4))
                    for u in range(nx // 2)
                    for v in range(ny // 2)
                ]
            )
            for core in range(2)
            for half in range(2)
        ]


def turned(members):
    return [members[-1 - i // 2 if i % 2 else i // 2] for i in range(len(members))]


def swapped(value, bit, plan):
    return lax.ppermute(value, AXES, [(i, i ^ bit) for i in range(plan.devices)])


def exchange(value, plan):
    shape = (plan.cells, plan.slots, plan.width)
    return lax.all_to_all(
        value.reshape(shape), AXES, split_axis=0, concat_axis=0, tiled=True, axis_index_groups=plan.groups
    ).reshape(plan.total, plan.width)


def call(kernel, out_shape, args, flops, moved, exps=0, after=(), scratch=(), limit=12, out_specs=None):
    return pl.pallas_call(
        kernel,
        out_shape=out_shape,
        in_specs=[VMEM] * len(args) + [ANY] * len(after),
        out_specs=out_specs or jax.tree.map(lambda _: VMEM, out_shape),
        scratch_shapes=list(scratch),
        compiler_params=pltpu.CompilerParams(vmem_limit_bytes=limit * 1024 * 1024),
        cost_estimate=pl.CostEstimate(flops=flops, bytes_accessed=moved, transcendentals=exps),
    )(*args, *after)


def iota(shape, dim):
    return lax.broadcasted_iota(I32, shape, dim)


def column(row):
    return jnp.broadcast_to(row, (LANES, row.shape[1])).T


def rows_dot(left, right):
    return lax.dot_general(left, right, (((1,), (1,)), ((), ())), preferred_element_type=F32)


def as_bf16(mask):
    return mask.astype(F32).astype(BF16)


def place_kernel(plan, bucket_ref, rows_ref, place_ref):
    nx, ny, files, slots = plan.nx, plan.ny, plan.files, plan.slots
    bucket = bucket_ref[...]
    low_b = ny.bit_length() - 1
    a = bucket >> (low_b + 1)
    b = (bucket >> 1) & (ny - 1)
    c = bucket & 1
    cell = (a & (nx // 2 - 1)) * (ny // 2) + (b & (ny // 2 - 1))
    tag = (a >> (nx.bit_length() - 2)) * 4 + (b >> (low_b - 1)) * 2 + c + 1
    order = cell * files + iota((1, files), 1)
    before = column(order)[:, :1] < order
    same = column(cell)[:, :1] == cell
    index = jnp.sum((before & same).astype(I32), axis=0, keepdims=True)
    over = (jnp.max(index, axis=1, keepdims=True) >= slots - 1).astype(F32)
    slot = jnp.where(index < slots - 1, cell * slots + index, plan.total)
    wide = rows_ref[...].astype(F32)
    square = jnp.sum(wide * wide, axis=1, keepdims=True)
    square = jnp.broadcast_to(square, (files, LANES)).T[0:1, :]
    inv = 1.0 / jnp.sqrt(square * (1.0 / plan.width) + epsilon)
    high = inv.astype(BF16).astype(F32)
    middle = (inv - high).astype(BF16).astype(F32)
    low = inv - high - middle
    line = iota((8, files), 0)
    place = jnp.zeros((8, files), F32)
    for index, value in enumerate((tag.astype(F32), high, middle, low, over, slot.astype(F32))):
        place = jnp.where(line == index, value, place)
    place_ref[...] = place


def pack_kernel(plan, place_ref, rows_ref, out_ref, info_ref):
    files, slots, known = plan.files, plan.slots, plan.known
    place = place_ref[...]
    facts = jnp.concatenate([place, jnp.zeros((TILE - 8, files), F32)], axis=0)
    facts = jnp.where(iota((TILE, files), 0) < FACTS, facts, 0.0).astype(BF16)
    over, slot = place[4:5, 0:LANES], place[5:6, :].astype(I32)
    match = as_bf16(iota((plan.total, files), 0) == slot)
    out_ref[...] = jnp.dot(match, rows_ref[...], preferred_element_type=F32).astype(BF16)
    info_ref[...] = jnp.zeros(info_ref.shape, F32)
    info_ref[0:8, 0:files] = place
    for block in range(plan.cells):
        line = rows_dot(facts, match[block * slots : (block + 1) * slots, :])
        row = slice(8 + block, 9 + block)
        for fact in range(FACTS):
            info_ref[row, fact * LANES : fact * LANES + known] = line[fact : fact + 1, :known]
        info_ref[row, FACTS * LANES : (FACTS + 1) * LANES] = over
    add_facts(plan, info_ref, out_ref)


def add_facts(plan, info_ref, out_ref):
    size = (FACTS + 1) * LANES
    last = iota((TILE, size), 0) == TILE - 1
    for block in range(plan.cells):
        end = (block + 1) * plan.slots
        tail = slice(end - TILE, end)
        out_ref[tail, 0:size] = jnp.where(
            last, info_ref[8 + block : 9 + block, 0:size], out_ref[tail, 0:size].astype(F32)
        ).astype(BF16)


def relay_kernel(plan, info_ref, rows_ref, after_ref, out_ref):
    del after_ref
    slot = info_ref[5:6, 0 : plan.files].astype(I32)
    match = as_bf16(iota((plan.total, plan.files), 0) == slot)
    out_ref[...] = jnp.dot(match, rows_ref[...], preferred_element_type=F32).astype(BF16)
    add_facts(plan, info_ref, out_ref)


def facts_of(plan, ref):
    slots, known = plan.slots, plan.known
    tags, invs, over = [], [], jnp.zeros((1, LANES), F32)
    for source in range(plan.cells):
        end = (source + 1) * slots
        lines = ref[end - TILE : end, 0 : (FACTS + 1) * LANES].astype(F32)[TILE - 1 : TILE, :]
        over = jnp.maximum(over, lines[:, FACTS * LANES :])
        tag, high, middle, low = (
            lines[:, fact * LANES : fact * LANES + known] for fact in range(FACTS)
        )
        tags.append(tag)
        invs.append(high + middle + low)
        if known < slots:
            empty = jnp.zeros((1, slots - known), F32)
            tags.append(empty)
            invs.append(empty)
    return jnp.concatenate(tags, axis=1), jnp.concatenate(invs, axis=1), over


def attend_kernel(plan, sets, olds, *refs):
    refs = list(refs)
    query_ref = refs.pop(0)
    keys = [(refs.pop(0), own) for own in sets]
    old_refs = refs[: 2 * olds]
    over_ref, out_ref, column_ref = refs[2 * olds :]
    total, width = plan.total, plan.width
    steps = 1 if total <= 1024 else 2
    chunk = total // steps
    tag, inv, over = facts_of(plan, query_ref)
    for old_over_ref in old_refs[0::2]:
        over = jnp.maximum(over, old_over_ref[0:1, :])
    place = jnp.maximum(tag.astype(I32) - 1, 0)
    bits = (2 << place) | (2 << (place ^ 1)) | (2 << (place ^ 2)) | (2 << (place ^ 4))
    bits = jnp.where(tag > 0.0, bits, 0)
    column_ref[0] = column(inv * (sharpness / width * math.log2(math.e)))
    column_ref[1] = column(bits.astype(F32))
    key_facts = []
    for key_ref, own in keys:
        key_tag, key_inv, key_over = facts_of(plan, key_ref)
        key_facts.append((1 << key_tag.astype(I32), key_inv))
        over = jnp.maximum(over, key_over)
    if olds:
        over_ref[0] = jnp.max(over).astype(I32)
    else:
        over_ref[...] = jnp.broadcast_to(over, over_ref.shape)
    for step in range(steps):
        here = slice(step * chunk, (step + 1) * chunk)
        query = query_ref[here, :]
        query_inv = column_ref[0, here, :][:, 0:1]
        query_bits = column_ref[1, here, :][:, 0:1].astype(I32)
        numerator, denominator = 0.0, 0.0
        for (key_ref, own), (key_bit, key_inv) in zip(keys, key_facts):
            score = rows_dot(query, key_ref[...]) * query_inv * key_inv
            live = (query_bits & key_bit) != 0
            if own:
                live = live & (iota((chunk, total), 0) + step * chunk != iota((chunk, total), 1))
            kernel = jnp.where(live, jnp.exp2(score), 0.0)
            denominator = denominator + jnp.sum(kernel, axis=1, keepdims=True)
            numerator = numerator + jnp.dot(
                kernel.astype(BF16), key_ref[...], preferred_element_type=F32
            )
        for old_ref in old_refs[1::2]:
            numerator = numerator + old_ref[here, 0:width]
            denominator = denominator + old_ref[here, width:][:, 0:1]
        if olds:
            out_ref[here, :] = (numerator / (1.0 + denominator)).astype(BF16)
        else:
            out_ref[here, 0:width] = numerator
            out_ref[here, width:] = jnp.broadcast_to(denominator, (chunk, LANES))


def attend(plan, query, key_sets, olds=(), weight=1):
    total, width = plan.total, plan.width
    count = len(key_sets) * total
    return call(
        functools.partial(attend_kernel, plan, [own for _, own in key_sets], len(olds)),
        (
            jax.ShapeDtypeStruct((1,), I32) if olds else jax.ShapeDtypeStruct((8, LANES), F32),
            jax.ShapeDtypeStruct((total, width), BF16)
            if olds
            else jax.ShapeDtypeStruct((total, width + LANES), F32),
        ),
        [query, *(rows for rows, _ in key_sets), *(part for old in olds for part in old)],
        weight * 4 * total * count * width,
        12 * total * width,
        total * count,
        scratch=[pltpu.VMEM((2, total, LANES), F32)],
        limit=26,
        out_specs=(SMEM if olds else VMEM, VMEM),
    )


def unpack_kernel(plan, place_ref, home_ref, out_ref):
    slot = column(place_ref[5:6, :])[:, 0:1].astype(I32)
    match = as_bf16(iota((plan.files, plan.total), 1) == slot)
    out_ref[...] = jnp.dot(match, home_ref[...], preferred_element_type=F32).astype(BF16)


def smooth(plan, embeddings, bucket):
    files, width, total = plan.files, plan.width, plan.total
    bucket = bucket.reshape(1, files)

    other_rows = swapped(embeddings, plan.half_bit, plan)
    place = call(
        functools.partial(place_kernel, plan),
        jax.ShapeDtypeStruct((8, files), F32),
        [bucket, embeddings],
        4 * files * files,
        2 * files * width,
    )
    payload, info = call(
        functools.partial(pack_kernel, plan),
        (
            jax.ShapeDtypeStruct((total, width), BF16),
            jax.ShapeDtypeStruct((8 + plan.cells, width), F32),
        ),
        [place, embeddings],
        2 * total * files * width,
        6 * files * width,
    )
    other_info = swapped(info, plan.half_bit, plan)
    own = lax.cond(
        lax.axis_index(AXES) != plan.devices, lambda payload: exchange(payload, plan), lambda payload: payload, payload
    )
    mate = swapped(own, plan.core_bit, plan)
    relayed = call(
        functools.partial(relay_kernel, plan),
        jax.ShapeDtypeStruct((total, width), BF16),
        [other_info, other_rows],
        2 * total * files * width,
        6 * files * width,
        after=(own,),
    )
    half = exchange(relayed, plan)
    near = attend(plan, own, [(own, True), (mate, False)])
    mate_half = swapped(half, plan.core_bit, plan)
    far = attend(plan, own, [(half, False)], weight=40)
    over, smoothed = attend(plan, own, [(mate_half, False)], [near, far])
    return smoothed, place, over[0] > 0


def unpack(plan, smoothed, place):
    home = exchange(smoothed, plan)
    return call(
        functools.partial(unpack_kernel, plan),
        jax.ShapeDtypeStruct((plan.files, plan.width), BF16),
        [place, home],
        2 * plan.total * plan.files * plan.width,
        6 * plan.files * plan.width,
    )


def body(embeddings, bucket):
    nx, ny = lax.axis_size("hx"), lax.axis_size("hy")
    most = 4 * BPD * CAP // (nx * ny)
    short, full = (
        Plan(nx, ny, *embeddings.shape, slots)
        for slots in (max(2 * TILE, most * 7 // 8 // TILE * TILE), most + TILE)
    )
    smoothed, place, over = smooth(short, embeddings, bucket)

    def again(smoothed, place):
        smoothed, place, _ = smooth(full, embeddings, bucket)
        return unpack(full, smoothed, place)

    return lax.cond(over, again, functools.partial(unpack, short), smoothed, place)


def solution(mesh):
    return jax.shard_map(
        body,
        mesh=mesh,
        in_specs=(P(("hx", "hy"), None), P(("hx", "hy"))),
        out_specs=P(("hx", "hy"), None),
        check_vma=False,
    )
```
